128 devices in a mesh: fsdp: 32 (over x, y, core), tp: 4 (over z).
Axes of the slice: x: 4, y: 4, z: 4, core: 2. Of those that a mesh axis runs over, the one named last changes fastest.
Arguments:
- gradient: float32 [8, 512, 14336], P(None, 'fsdp', 'tp'), may hold values from -200 to 200
- first_moment: float32 [64, 512, 2048], P('fsdp', None, 'tp'), may hold values from -4 to 4
- second_moment: float32 [64, 512, 2048], P('fsdp', None, 'tp'), may hold values from 0.01 to 1
- left_basis: float32 [64, 512, 2048], P('fsdp', None, 'tp'), may hold values from -0.25 to 0.25
- right_basis: float32 [64, 512, 2048], P('fsdp', None, 'tp'), may hold values from -0.25 to 0.25
- left_gram: float32 [64, 512, 2048], P('fsdp', None, 'tp'), may hold values from -6 to 6
- right_gram: float32 [64, 512, 2048], P('fsdp', None, 'tp'), may hold values from -6 to 6
- owner_slot: int32 [8, 28], P(None, 'tp'), may hold values from 0 to 63, as said below
Outputs:
- direction: float32 [8, 512, 14336], P(None, 'fsdp', 'tp')
- new_first: float32 [64, 512, 2048], P('fsdp', None, 'tp')
- new_second: float32 [64, 512, 2048], P('fsdp', None, 'tp')
- new_left_gram: float32 [64, 512, 2048], P('fsdp', None, 'tp')
- new_right_gram: float32 [64, 512, 2048], P('fsdp', None, 'tp')
The draws below stay inside these ranges and needn't reach their ends.
Inputs may be any that keep to these rules, and one draw needn't show every extreme that they name: `owner_slot`: within the 7 block columns of one index of tp, all entries are distinct; slot s lies on index s // 2 of fsdp.
All inputs are finite; a program needn't handle non-finite values.
Results may differ from the reference program's by a relative error of at most 0.00007.
Values sent between devices are 32-bit elements; how exact they have to be, the bound alone decides.
A program may use at most 128 MiB of HBM per device.

```python
import math
import jax
import jax.numpy as jnp
from jax import lax

D = 4096
FF = 14336
BLK = 512
RB = 8
CB = 28
CB_DEV = 7
SLOTS = 64
N_TP = 4


def draw_gradient(key, part):
    key = jax.random.fold_in(key, 11)
    key_base, key_rows, key_cols = jax.random.split(key, 3)
    base = jnp.clip(jax.random.normal(key_base, (RB, BLK, FF), jnp.float32), -6.0, 6.0)
    row_log = jax.random.uniform(key_rows, (RB, BLK, 1), jnp.float32, 0.0, 1.15)
    col_log = jax.random.uniform(key_cols, (1, 1, FF), jnp.float32, 0.0, 1.15)
    inside = jnp.arange(BLK, dtype=jnp.float32).reshape(1, BLK, 1) / BLK
    across = jnp.arange(FF, dtype=jnp.float32).reshape(1, 1, FF) / FF
    scaling = jnp.exp(row_log + col_log) * jnp.sqrt((1.0 + 2.0 * inside) * (1.0 + 2.0 * across))
    return base * scaling


def owner_column(key):
    used = RB * CB_DEV
    key_empty, key_order = jax.random.split(key)
    inner = jax.random.permutation(key_empty, SLOTS - 2) + 1
    marked = jnp.zeros((SLOTS,), jnp.int32).at[inner[:SLOTS - used]].set(1)
    chosen = jnp.argsort(marked, stable=True)[:used].astype(jnp.int32)
    return chosen[jax.random.permutation(key_order, used)]


def draw_owner_slot(key, part):
    key = jax.random.fold_in(key, 5)
    column_keys = jax.random.split(key, N_TP)
    columns = jax.vmap(owner_column)(column_keys)
    return columns.reshape(N_TP, RB, CB_DEV).transpose(1, 0, 2).reshape(RB, CB).astype(jnp.int32)


def block_scale(own_key, extent, shards, low, high):
    gain = 1.0
    for dim, shards_of in shards:
        heights = jax.random.uniform(jax.random.fold_in(jax.random.fold_in(own_key, 6), dim), (shards_of,), jnp.float32, low / len(shards), high / len(shards))
        gain = gain * jnp.repeat(jnp.exp(heights), extent[dim] // shards_of).reshape((-1,) + (1,) * (len(extent) - 1 - dim))
    return gain


def scatter_about(rng, shape, scale, limit, cuts=(), kind=jnp.bfloat16):
    entries = jax.random.normal(rng, shape, jnp.float32) * scale
    if len(cuts) > 0:
        entries = block_scale(rng, shape, cuts, -0.22, 0.18) * entries
    return jnp.clip(entries, min=-limit, max=limit).astype(kind)


def setup_inputs(seed: int = 0) -> dict:
    splits = jax.random.split(jax.random.key(seed), 9)
    return {
        "gradient": draw_gradient(jax.random.fold_in(splits[8], 71), 0),
        "first_moment": scatter_about(splits[1], (SLOTS, BLK, N_TP * BLK), 0.5, 4.0, ((0, 32), (2, 4)), jnp.float32),
        "second_moment": jnp.clip(jnp.exp(math.log(1.0) - 4.6051702 * jax.random.uniform(splits[2], (SLOTS, BLK, N_TP * BLK), jnp.float32) ** block_scale(splits[2], (SLOTS, BLK, N_TP * BLK), ((0, 32), (2, 4)), -0.2, 0.2)), 0.01, 1.0),
        "left_basis": scatter_about(splits[3], (SLOTS, BLK, N_TP * BLK), BLK ** -0.5, 0.25, ((0, 32), (2, 4)), jnp.float32),
        "right_basis": scatter_about(splits[4], (SLOTS, BLK, N_TP * BLK), BLK ** -0.5, 0.25, ((0, 32), (2, 4)), jnp.float32),
        "left_gram": scatter_about(splits[5], (SLOTS, BLK, N_TP * BLK), 1.0, 6.0, ((0, 32), (2, 4)), jnp.float32),
        "right_gram": scatter_about(splits[6], (SLOTS, BLK, N_TP * BLK), 1.0, 6.0, ((0, 32), (2, 4)), jnp.float32),
        "owner_slot": draw_owner_slot(jax.random.fold_in(splits[8], 71), 0),
    }


first_beta = 0.9
second_beta = 0.95
gram_beta = 0.95
first_fix = 1.0 / (1.0 - 0.9 ** 10)
second_fix = 1.0 / (1.0 - 0.95 ** 10)
eps_value = 1e-08

def advance(grad_block, first_state, second_state, left_basis, right_basis, left_stat, right_stat, clip_scale):
    highest = lax.Precision.HIGHEST
    partial_value = jnp.dot(left_basis.T, grad_block, precision=highest, preferred_element_type=jnp.float32)
    rotated = clip_scale * jnp.dot(partial_value, right_basis, precision=highest, preferred_element_type=jnp.float32)
    first_next = first_beta * first_state + (1.0 - first_beta) * rotated
    second_next = second_beta * second_state + (1.0 - second_beta) * rotated * rotated
    normalized = first_fix * first_next / (jnp.sqrt(second_fix * second_next) + eps_value)
    leftside = jnp.dot(left_basis, normalized, precision=highest, preferred_element_type=jnp.float32)
    rotated_back = jnp.dot(leftside, right_basis.T, precision=highest, preferred_element_type=jnp.float32)
    gram_scale = clip_scale * clip_scale / grad_block.shape[0]
    left_next = gram_beta * left_stat + (1.0 - gram_beta) * gram_scale * jnp.dot(grad_block, grad_block.T, precision=highest, preferred_element_type=jnp.float32)
    right_next = gram_beta * right_stat + (1.0 - gram_beta) * gram_scale * jnp.dot(grad_block.T, grad_block, precision=highest, preferred_element_type=jnp.float32)
    return (rotated_back, first_next, second_next, left_next, right_next)

def advance_packed(packed):
    return advance(*packed, 1.0)

def split_state(state):
    return state.reshape(SLOTS, BLK, N_TP, BLK).transpose(0, 2, 1, 3).reshape(SLOTS * N_TP, BLK, BLK)

def join_state(state):
    return state.reshape(SLOTS, N_TP, BLK, BLK).transpose(0, 2, 1, 3).reshape(SLOTS, BLK, N_TP * BLK)

def reference(gradient, first_moment, second_moment, left_basis, right_basis, left_gram, right_gram, owner_slot):
    norm_sq = jnp.sum(gradient * gradient)
    factor = jnp.minimum(1.0, math.sqrt(D * FF) / jnp.sqrt(norm_sq))
    clipped = gradient * factor
    blocks = clipped.reshape(RB, BLK, CB, BLK).transpose(0, 2, 1, 3).reshape(RB * CB, BLK, BLK)
    column = jnp.arange(CB, dtype=jnp.int32) // CB_DEV
    column = jnp.broadcast_to(column[None, :], (RB, CB)).reshape(-1)
    slot_flat = owner_slot.reshape(-1).astype(jnp.int32)
    slotted = jnp.zeros((SLOTS, N_TP, BLK, BLK), gradient.dtype).at[slot_flat, column].set(blocks)
    packed = (slotted.reshape(SLOTS * N_TP, BLK, BLK), split_state(first_moment), split_state(second_moment), split_state(left_basis), split_state(right_basis), split_state(left_gram), split_state(right_gram))
    rotated_back, first_next, second_next, left_next, right_next = lax.map(advance_packed, packed)
    picked = rotated_back.reshape(SLOTS, N_TP, BLK, BLK)[slot_flat, column]
    direction = picked.reshape(RB, CB, BLK, BLK).transpose(0, 2, 1, 3).reshape(RB, BLK, FF)
    return (direction, join_state(first_next), join_state(second_next), join_state(left_next), join_state(right_next))
```

```python
import functools
import math

import jax
import jax.numpy as jnp
from jax import lax
from jax.experimental import pallas as pl
from jax.experimental.pallas import tpu as pltpu
from jax.sharding import PartitionSpec as P

D = 4096
FF = 14336

first_beta = 0.9
second_beta = 0.95
gram_beta = 0.95
first_fix = 1.0 / (1.0 - 0.9**10)
second_fix = 1.0 / (1.0 - 0.95**10)
eps_value = 1e-08

MESH = pl.DeviceIdType.MESH
f32 = jnp.float32
bf16 = jnp.bfloat16

CHIP_STEPS = (
    (2, 2),
    (3, 2), (2, 3), (1, 2), (2, 1),
    (0, 2), (2, 0),
    (3, 1), (1, 3), (3, 3), (1, 1),
    (0, 3), (0, 1), (3, 0), (1, 0),
)
STEPS = tuple((a, b, c) for c in (0, 1) for a, b in CHIP_STEPS) + ((0, 0, 1),)
ROW_STEPS = (2, 1, 3, 0)


def split(value):
    high = value.astype(bf16)
    return high, (value - high.astype(f32)).astype(bf16)


def put(pair, rows, value):
    high, low = split(value)
    pair[0, rows, :] = high
    pair[1, rows, :] = low


def product(left, rows, right):
    left_high, left_low = left[0, rows, :], left[1, rows, :]
    right_high, right_low = right[0], right[1]
    total = jnp.dot(left_low, right_high, preferred_element_type=f32)
    total += jnp.dot(left_high, right_low, preferred_element_type=f32)
    return total + jnp.dot(left_high, right_high, preferred_element_type=f32)


def kernel(
    block_at, owner, gradient, first_in, second_in, left_in, right_in, left_stat, right_stat,
    direction, first_out, second_out, left_out, right_out,
    grad, packed, arrived, leaving, returned, gathered,
    first, second, left_raw, right_raw, left_gram, right_gram,
    left_basis, left_turned, right_basis, right_turned,
    block, turned, partial, normal, rotated,
    column_parts, row_parts, mine, factor,
    fetch_sem, load_sem, store_sem, column_send, column_recv, norm_send, norm_recv, in_send, in_recv, out_send, out_recv,
):
    devices, cols, size = 32, owner.shape[1], 512
    me = lax.axis_index("fsdp")
    tp = lax.axis_index("tp")
    my_x, my_y, my_core = me // 8, (me // 2) % 4, me % 2

    def place(step):
        a, b, c = step
        return ((my_x + a) % 4) * 8 + ((my_y + b) % 4) * 2 + (my_core + c) % 2

    loads = [
        pltpu.make_async_copy(source, target, load_sem.at[i])
        for i, (source, target) in enumerate((
            (left_in, left_raw), (right_in, right_raw), (first_in, first),
            (second_in, second), (left_stat, left_gram), (right_stat, right_gram),
        ))
    ]
    rows_b = gradient.shape[0]
    fetches = [
        pltpu.make_async_copy(
            gradient.at[:, :, pl.ds(c * size, size)], grad.at[pl.ds(c * rows_b, rows_b)], fetch_sem.at[c]
        )
        for c in range(cols)
    ]
    for fetch in fetches:
        fetch.start()
    grad[cols * rows_b] = jnp.zeros(grad.shape[1:], f32)

    barrier = pltpu.get_barrier_semaphore()

    def greet(k, _):
        pl.semaphore_signal(barrier, inc=1, device_id={"fsdp": (me + k) % devices}, device_id_type=MESH)
        return 0

    def greet_column(k, _):
        pl.semaphore_signal(barrier, inc=1, device_id={"tp": (tp + k) % 4}, device_id_type=MESH)
        return 0

    lax.fori_loop(1, devices, greet, 0)
    lax.fori_loop(1, 4, greet_column, 0)
    for fetch in fetches:
        fetch.wait()
    for load in loads:
        load.start()

    def pack(d, total):
        for s in (0, 1):
            value = grad[block_at[2 * d + s]]
            packed[s, d] = value
            total = total + value * value
        return total

    total = lax.fori_loop(0, devices, pack, jnp.zeros((16, size), f32))
    total = total[:8] + total[8:]
    total = total[:, 0:128] + total[:, 128:256] + total[:, 256:384] + total[:, 384:512]
    mine[0] = total
    column_parts[tp] = total
    for s in (0, 1):
        arrived[s, me] = packed[s, me]

    pl.semaphore_wait(barrier, devices - 1 + 3)

    def column_copy(k):
        return pltpu.make_async_remote_copy(
            src_ref=mine.at[0], dst_ref=column_parts.at[tp],
            send_sem=column_send.at[k], recv_sem=column_recv.at[k],
            device_id={"tp": (tp + k + 1) % 4}, device_id_type=MESH,
        )

    def in_copy(s, k):
        to = place(STEPS[k])
        return pltpu.make_async_remote_copy(
            src_ref=packed.at[s, to], dst_ref=arrived.at[s, me],
            send_sem=in_send.at[s, k], recv_sem=in_recv.at[s, k],
            device_id={"fsdp": to}, device_id_type=MESH,
        )

    def norm_copy(k):
        return pltpu.make_async_remote_copy(
            src_ref=mine.at[1], dst_ref=row_parts.at[me],
            send_sem=norm_send.at[k], recv_sem=norm_recv.at[k],
            device_id={"fsdp": place(STEPS[k])}, device_id_type=MESH,
        )

    def out_copy(s, a, b, c):
        to = ((my_x + a) % 4) * 8 + ((my_y + b) % 4) * 2 + (my_core + c) % 2
        k = (a * 4 + b) * 2 + c
        return pltpu.make_async_remote_copy(
            src_ref=leaving.at[s, to], dst_ref=returned.at[2 * me + s],
            send_sem=out_send.at[s, k], recv_sem=out_recv.at[s, k],
            device_id={"fsdp": to}, device_id_type=MESH,
        )

    for k in range(3):
        column_copy(k).start()
    for k in range(len(STEPS)):
        in_copy(0, k).start()
    for k in range(3):
        column_copy(k).wait()
    own = column_parts[0] + column_parts[1] + column_parts[2] + column_parts[3]
    mine[1] = own
    row_parts[me] = own
    for k in range(len(STEPS)):
        norm_copy(k).start()
    for k in range(len(STEPS)):
        in_copy(1, k).start()

    loads[0].wait()
    loads[1].wait()

    def prepare(s, _):
        rows = pl.ds(0, size)
        left = left_raw[s]
        put(left_basis.at[s], rows, left)
        put(left_turned.at[s], rows, left.T)
        right = right_raw[s]
        put(right_basis.at[s], rows, right)
        put(right_turned.at[s], rows, right.T)
        return 0

    lax.fori_loop(0, 2, prepare, 0)
    for load in loads[2:]:
        load.wait()

    def piece(s, t):
        return arrived[s, pl.ds(t * 16, 16)].reshape(256, size)

    def rotate(s):
        for k in range(len(STEPS)):
            in_copy(s, k).wait()
        for t in range(2):
            put(block, pl.ds(t * 256, 256), piece(s, t))

        def to_partial(t, _):
            rows = pl.ds(pl.multiple_of(t * 256, 256), 256)
            put(partial, rows, product(left_turned.at[s], rows, block))
            return 0

        lax.fori_loop(0, 2, to_partial, 0)

        def to_rotated(t, _):
            rows = pl.ds(pl.multiple_of(t * 256, 256), 256)
            rotated[rows, :] = product(partial, rows, right_basis.at[s])
            return 0

        lax.fori_loop(0, 2, to_rotated, 0)

    def finish_norm():
        for k in range(len(STEPS)):
            norm_copy(k).wait()
        parts = row_parts[0]
        for d in range(1, devices):
            parts = parts + row_parts[d]
        norm_sq = jnp.sum(jnp.sum(parts, axis=0, keepdims=True), axis=1, keepdims=True)
        scale = jnp.minimum(1.0, math.sqrt(D * FF) / jnp.sqrt(norm_sq))
        factor[...] = jnp.broadcast_to(scale, factor.shape)

    def rest(s):
        def update(t, _):
            rows = pl.ds(pl.multiple_of(t * 64, 64), 64)
            turn = rotated[rows, :] * factor[0:1, :]
            first_next = first_beta * first[s, rows, :] + (1.0 - first_beta) * turn
            second_next = second_beta * second[s, rows, :] + (1.0 - second_beta) * turn * turn
            first[s, rows, :] = first_next
            second[s, rows, :] = second_next
            put(normal, rows, first_fix * first_next / (jnp.sqrt(second_fix * second_next) + eps_value))
            return 0

        lax.fori_loop(0, size // 64, update, 0)
        pltpu.make_async_copy(first.at[s], first_out.at[s], store_sem.at[0, s]).start()
        pltpu.make_async_copy(second.at[s], second_out.at[s], store_sem.at[1, s]).start()

        def to_partial(t, _):
            rows = pl.ds(pl.multiple_of(t * 256, 256), 256)
            put(partial, rows, product(left_basis.at[s], rows, normal))
            return 0

        lax.fori_loop(0, 2, to_partial, 0)

        for a in ROW_STEPS:
            to_x = (my_x + a) % 4
            rows = pl.ds(pl.multiple_of(to_x * 128, 128), 128)
            leaving[s, pl.ds(to_x * 8, 8)] = product(partial, rows, right_turned.at[s]).reshape(8, 16, size)
            for c in (0, 1):
                for b in ROW_STEPS:
                    if (a, b, c) != (0, 0, 0):
                        out_copy(s, a, b, c).start()
        returned[2 * me + s] = leaving[s, me]

    rotate(0)
    finish_norm()
    rest(0)
    rotate(1)
    rest(1)

    gram_scale = factor[0:1, :] * factor[0:1, :] * ((1.0 - gram_beta) / size)
    def grams(s, _):
        def load(t, _):
            rows = pl.ds(pl.multiple_of(t * 256, 256), 256)
            put(block, rows, piece(s, t))
            return 0

        lax.fori_loop(0, 2, load, 0)
        put(turned, pl.ds(0, size), arrived[s].reshape(size, size).T)

        def step(t, _):
            rows = pl.ds(pl.multiple_of(t * 256, 256), 256)
            left_gram[s, rows, :] = gram_beta * left_gram[s, rows, :] + gram_scale * product(block, rows, turned)
            right_gram[s, rows, :] = gram_beta * right_gram[s, rows, :] + gram_scale * product(turned, rows, block)
            return 0

        lax.fori_loop(0, 2, step, 0)
        return 0

    lax.fori_loop(0, 2, grams, 0)
    stores = [
        pltpu.make_async_copy(left_gram, left_out, store_sem.at[2, 0]),
        pltpu.make_async_copy(right_gram, right_out, store_sem.at[3, 0]),
    ]
    for store in stores:
        store.start()

    for s in (0, 1):
        for a in ROW_STEPS:
            for c in (0, 1):
                for b in ROW_STEPS:
                    if (a, b, c) != (0, 0, 0):
                        out_copy(s, a, b, c).wait()

    def unpack(i, _):
        for c in range(cols):
            gathered[i, :, c * size:(c + 1) * size] = returned[owner[i, c]]
        return 0

    lax.fori_loop(0, gathered.shape[0], unpack, 0)
    last = pltpu.make_async_copy(gathered, direction, store_sem.at[2, 1])
    last.start()
    for s in (0, 1):
        pltpu.make_async_copy(first.at[s], first_out.at[s], store_sem.at[0, s]).wait()
        pltpu.make_async_copy(second.at[s], second_out.at[s], store_sem.at[1, s]).wait()
    for store in stores:
        store.wait()
    last.wait()


def local(gradient, first_moment, second_moment, left_basis, right_basis, left_gram, right_gram, owner_slot):
    rows_b, sub_rows, width = gradient.shape
    slots_dev, size, _ = first_moment.shape
    devices = lax.axis_size("fsdp")
    cols = width // size
    slots = lax.broadcasted_iota(jnp.int32, (devices * slots_dev, rows_b, cols), 0)
    i = lax.broadcasted_iota(jnp.int32, slots.shape, 1)
    c = lax.broadcasted_iota(jnp.int32, slots.shape, 2)
    blocks = rows_b * cols
    block_at = blocks + jnp.sum(jnp.where(owner_slot[None] == slots, c * rows_b + i - blocks, 0), axis=(1, 2))
    state = jax.ShapeDtypeStruct(first_moment.shape, f32)
    hbm = pl.BlockSpec(memory_space=pl.ANY)
    smem = pl.BlockSpec(memory_space=pltpu.SMEM)
    pieces = pltpu.VMEM((slots_dev, devices, sub_rows, size), f32)
    whole = pltpu.VMEM(first_moment.shape, f32)
    pair = pltpu.VMEM((2, size, size), bf16)
    pairs = pltpu.VMEM((slots_dev, 2, size, size), bf16)
    n = len(STEPS)
    dma = pltpu.SemaphoreType.DMA
    return pl.pallas_call(
        kernel,
        out_shape=(jax.ShapeDtypeStruct(gradient.shape, f32), state, state, state, state),
        in_specs=[smem, smem] + [hbm] * 7,
        out_specs=(hbm,) * 5,
        scratch_shapes=[
            pltpu.VMEM((blocks + 1, sub_rows, size), f32), pieces, pieces, pieces,
            pltpu.VMEM((devices * slots_dev, sub_rows, size), f32), pltpu.VMEM(gradient.shape, f32),
            whole, whole, whole, whole, whole, whole,
            pairs, pairs, pairs, pairs,
            pair, pair, pair, pair, pltpu.VMEM((size, size), f32),
            pltpu.VMEM((4, 8, 128), f32), pltpu.VMEM((devices, 8, 128), f32),
            pltpu.VMEM((2, 8, 128), f32), pltpu.VMEM((8, size), f32),
            dma((cols,)), dma((6,)), dma((4, 2)), dma((3,)), dma((3,)), dma((n,)), dma((n,)),
            dma((2, n)), dma((2, n)), dma((2, n + 1)), dma((2, n + 1)),
        ],
        compiler_params=pltpu.CompilerParams(
            collective_id=0, has_side_effects=True, vmem_limit_bytes=60 * 1024 * 1024
        ),
    )(block_at, owner_slot, gradient, first_moment, second_moment, left_basis, right_basis, left_gram, right_gram)


def solution(mesh):
    in_specs = (
        P(None, "fsdp", "tp"),
        P("fsdp", None, "tp"),
        P("fsdp", None, "tp"),
        P("fsdp", None, "tp"),
        P("fsdp", None, "tp"),
        P("fsdp", None, "tp"),
        P("fsdp", None, "tp"),
        P(None, "tp"),
    )
    out_specs = (
        P(None, "fsdp", "tp"),
        P("fsdp", None, "tp"),
        P("fsdp", None, "tp"),
        P("fsdp", None, "tp"),
        P("fsdp", None, "tp"),
    )
    return jax.shard_map(local, mesh=mesh, in_specs=in_specs, out_specs=out_specs, check_vma=False)
```

```python
import functools
import math

import jax
import jax.numpy as jnp
from jax import lax
from jax.experimental import pallas as pl
from jax.experimental.pallas import tpu as pltpu
from jax.sharding import PartitionSpec as P

D = 4096
FF = 14336

first_beta = 0.9
second_beta = 0.95
gram_beta = 0.95
first_fix = 1.0 / (1.0 - 0.9**10)
second_fix = 1.0 / (1.0 - 0.95**10)
eps_value = 1e-08

MESH = pl.DeviceIdType.MESH
f32 = jnp.float32
bf16 = jnp.bfloat16

CHIP_STEPS = (
    (2, 2),
    (3, 2), (2, 3), (1, 2), (2, 1),
    (0, 2), (2, 0),
    (3, 1), (1, 3), (3, 3), (1, 1),
    (0, 3), (0, 1), (3, 0), (1, 0),
)
STEPS = tuple((a, b, c) for c in (0, 1) for a, b in CHIP_STEPS) + ((0, 0, 1),)
ROW_STEPS = (2, 1, 3, 0)


def split(value):
    high = value.astype(bf16)
    return high, (value - high.astype(f32)).astype(bf16)


def put(pair, rows, value):
    high, low = split(value)
    pair[0, rows, :] = high
    pair[1, rows, :] = low


def product(left, rows, right):
    left_high, left_low = left[0, rows, :], left[1, rows, :]
    right_high, right_low = right[0], right[1]
    total = jnp.dot(left_low, right_high, preferred_element_type=f32)
    total += jnp.dot(left_high, right_low, preferred_element_type=f32)
    return total + jnp.dot(left_high, right_high, preferred_element_type=f32)


def kernel(
    owner_in, gradient, first_in, second_in, left_in, right_in, left_stat, right_stat,
    returned, first, second, left_gram, right_gram,
    grad, packed, arrived, leaving, owner, places, block_at,
    left_raw, right_raw,
    left_basis, left_turned, right_basis, right_turned,
    block, turned, partial, normal, rotated,
    column_parts, row_parts, mine, factor,
    fetch_sem, place_sem, load_sem, column_send, column_recv, norm_send, norm_recv, in_send, in_recv, out_send, out_recv,
):
    devices, cols, size = 32, owner_in.shape[1], 512
    me = lax.axis_index("fsdp")
    tp = lax.axis_index("tp")
    my_x, my_y, my_core = me // 8, (me // 2) % 4, me % 2

    def place(step):
        a, b, c = step
        return ((my_x + a) % 4) * 8 + ((my_y + b) % 4) * 2 + (my_core + c) % 2

    loads = [
        pltpu.make_async_copy(source, target, load_sem.at[i])
        for i, (source, target) in enumerate((
            (left_in, left_raw), (right_in, right_raw), (first_in, first),
            (second_in, second), (left_stat, left_gram), (right_stat, right_gram),
        ))
    ]
    rows_b = gradient.shape[0]
    blocks = rows_b * cols
    fetches = [
        pltpu.make_async_copy(
            gradient.at[:, :, pl.ds(c * size, size)], grad.at[pl.ds(c * rows_b, rows_b)], fetch_sem.at[c]
        )
        for c in range(cols)
    ]
    fetch_owner = pltpu.make_async_copy(owner_in, owner, place_sem.at[1])
    fetch_owner.start()
    for fetch in fetches:
        fetch.start()
    grad[blocks] = jnp.zeros(grad.shape[1:], f32)

    barrier = pltpu.get_barrier_semaphore()

    def greet(k, _):
        pl.semaphore_signal(barrier, inc=1, device_id={"fsdp": (me + k) % devices}, device_id_type=MESH)
        return 0

    def greet_column(k, _):
        pl.semaphore_signal(barrier, inc=1, device_id={"tp": (tp + k) % 4}, device_id_type=MESH)
        return 0

    lax.fori_loop(1, devices, greet, 0)
    lax.fori_loop(1, 4, greet_column, 0)
    fetch_owner.wait()
    slots = lax.broadcasted_iota(jnp.int32, (rows_b, 128), 1)
    row = lax.broadcasted_iota(jnp.int32, (rows_b, 128), 0)
    found = jnp.full((rows_b, 128), -1, jnp.int32)
    for c in range(cols):
        found = jnp.maximum(found, jnp.where(owner[:, c:c + 1] == slots, row + c * rows_b, -1))
    found = jnp.max(found, axis=0, keepdims=True)
    found = jnp.where(found < 0, blocks, found)
    places[...] = jnp.broadcast_to(found, places.shape)
    to_scalars = pltpu.make_async_copy(places, block_at, place_sem.at[0])
    to_scalars.start()
    to_scalars.wait()
    for fetch in fetches:
        fetch.wait()
    for load in loads:
        load.start()

    def pack(d, total):
        for s in (0, 1):
            value = grad[block_at[0, 2 * d + s]]
            packed[s, d] = value
            total = total + value * value
        return total

    total = lax.fori_loop(0, devices, pack, jnp.zeros((16, size), f32))
    total = total[:8] + total[8:]
    total = total[:, 0:128] + total[:, 128:256] + total[:, 256:384] + total[:, 384:512]
    mine[0] = total
    column_parts[tp] = total
    for s in (0, 1):
        arrived[s, me] = packed[s, me]

    pl.semaphore_wait(barrier, devices - 1 + 3)

    def column_copy(k):
        return pltpu.make_async_remote_copy(
            src_ref=mine.at[0], dst_ref=column_parts.at[tp],
            send_sem=column_send.at[k], recv_sem=column_recv.at[k],
            device_id={"tp": (tp + k + 1) % 4}, device_id_type=MESH,
        )

    def in_copy(s, k):
        to = place(STEPS[k])
        return pltpu.make_async_remote_copy(
            src_ref=packed.at[s, to], dst_ref=arrived.at[s, me],
            send_sem=in_send.at[s, k], recv_sem=in_recv.at[s, k],
            device_id={"fsdp": to}, device_id_type=MESH,
        )

    def norm_copy(k):
        return pltpu.make_async_remote_copy(
            src_ref=mine.at[1], dst_ref=row_parts.at[me],
            send_sem=norm_send.at[k], recv_sem=norm_recv.at[k],
            device_id={"fsdp": place(STEPS[k])}, device_id_type=MESH,
        )

    def out_copy(s, a, b, c):
        to = ((my_x + a) % 4) * 8 + ((my_y + b) % 4) * 2 + (my_core + c) % 2
        k = (a * 4 + b) * 2 + c
        return pltpu.make_async_remote_copy(
            src_ref=leaving.at[s, to], dst_ref=returned.at[2 * me + s],
            send_sem=out_send.at[s, k], recv_sem=out_recv.at[s, k],
            device_id={"fsdp": to}, device_id_type=MESH,
        )

    for k in range(3):
        column_copy(k).start()
    for k in range(len(STEPS)):
        in_copy(0, k).start()
    for k in range(3):
        column_copy(k).wait()
    own = column_parts[0] + column_parts[1] + column_parts[2] + column_parts[3]
    mine[1] = own
    row_parts[me] = own
    for k in range(len(STEPS)):
        norm_copy(k).start()
    for k in range(len(STEPS)):
        in_copy(1, k).start()

    loads[0].wait()
    loads[1].wait()

    def prepare(s, _):
        rows = pl.ds(0, size)
        left = left_raw[s]
        put(left_basis.at[s], rows, left)
        put(left_turned.at[s], rows, left.T)
        right = right_raw[s]
        put(right_basis.at[s], rows, right)
        put(right_turned.at[s], rows, right.T)
        return 0

    lax.fori_loop(0, 2, prepare, 0)
    for load in loads[2:]:
        load.wait()

    def piece(s, t):
        return arrived[s, pl.ds(t * 16, 16)].reshape(256, size)

    def rotate(s):
        for k in range(len(STEPS)):
            in_copy(s, k).wait()
        for t in range(2):
            put(block, pl.ds(t * 256, 256), piece(s, t))

        def to_partial(t, _):
            rows = pl.ds(pl.multiple_of(t * 256, 256), 256)
            put(partial, rows, product(left_turned.at[s], rows, block))
            return 0

        lax.fori_loop(0, 2, to_partial, 0)

        def to_rotated(t, _):
            rows = pl.ds(pl.multiple_of(t * 256, 256), 256)
            rotated[rows, :] = product(partial, rows, right_basis.at[s])
            return 0

        lax.fori_loop(0, 2, to_rotated, 0)

    def finish_norm():
        for k in range(len(STEPS)):
            norm_copy(k).wait()
        parts = row_parts[0]
        for d in range(1, devices):
            parts = parts + row_parts[d]
        norm_sq = jnp.sum(jnp.sum(parts, axis=0, keepdims=True), axis=1, keepdims=True)
        scale = jnp.minimum(1.0, math.sqrt(D * FF) / jnp.sqrt(norm_sq))
        factor[...] = jnp.broadcast_to(scale, factor.shape)

    def rest(s):
        def update(t, _):
            rows = pl.ds(pl.multiple_of(t * 64, 64), 64)
            turn = rotated[rows, :] * factor[0:1, :]
            first_next = first_beta * first[s, rows, :] + (1.0 - first_beta) * turn
            second_next = second_beta * second[s, rows, :] + (1.0 - second_beta) * turn * turn
            first[s, rows, :] = first_next
            second[s, rows, :] = second_next
            put(normal, rows, first_fix * first_next / (jnp.sqrt(second_fix * second_next) + eps_value))
            return 0

        lax.fori_loop(0, size // 64, update, 0)

        def to_partial(t, _):
            rows = pl.ds(pl.multiple_of(t * 256, 256), 256)
            put(partial, rows, product(left_basis.at[s], rows, normal))
            return 0

        lax.fori_loop(0, 2, to_partial, 0)

        for a in ROW_STEPS:
            to_x = (my_x + a) % 4
            rows = pl.ds(pl.multiple_of(to_x * 128, 128), 128)
            leaving[s, pl.ds(to_x * 8, 8)] = product(partial, rows, right_turned.at[s]).reshape(8, 16, size)
            for c in (0, 1):
                for b in ROW_STEPS:
                    if (a, b, c) != (0, 0, 0):
                        out_copy(s, a, b, c).start()
        returned[2 * me + s] = leaving[s, me]

    rotate(0)
    finish_norm()
    rest(0)
    rotate(1)
    rest(1)

    gram_scale = factor[0:1, :] * factor[0:1, :] * ((1.0 - gram_beta) / size)
    def grams(s, _):
        def load(t, _):
            rows = pl.ds(pl.multiple_of(t * 256, 256), 256)
            put(block, rows, piece(s, t))
            return 0

        lax.fori_loop(0, 2, load, 0)
        put(turned, pl.ds(0, size), arrived[s].reshape(size, size).T)

        def step(t, _):
            rows = pl.ds(pl.multiple_of(t * 256, 256), 256)
            left_gram[s, rows, :] = gram_beta * left_gram[s, rows, :] + gram_scale * product(block, rows, turned)
            right_gram[s, rows, :] = gram_beta * right_gram[s, rows, :] + gram_scale * product(turned, rows, block)
            return 0

        lax.fori_loop(0, 2, step, 0)
        return 0

    lax.fori_loop(0, 2, grams, 0)

    for s in (0, 1):
        for a in ROW_STEPS:
            for c in (0, 1):
                for b in ROW_STEPS:
                    if (a, b, c) != (0, 0, 0):
                        out_copy(s, a, b, c).wait()


def store(
    owner_in, returned, first, second, left_gram, right_gram,
    direction, first_out, second_out, left_out, right_out,
    owner, owner_sem, sem, block_sem,
):
    rows_b, cols = owner_in.shape
    size = returned.shape[2]
    copies = [
        pltpu.make_async_copy(source, target, sem.at[i])
        for i, (source, target) in enumerate(
            ((first, first_out), (second, second_out), (left_gram, left_out), (right_gram, right_out))
        )
    ]

    def pick(i, c):
        return pltpu.make_async_copy(
            returned.at[owner[i, c]], direction.at[i, :, pl.ds(c * size, size)], block_sem.at[i, c]
        )

    fetch_owner = pltpu.make_async_copy(owner_in, owner, owner_sem.at[0])
    fetch_owner.start()
    for copy in copies:
        copy.start()
    fetch_owner.wait()
    for i in range(rows_b):
        for c in range(cols):
            pick(i, c).start()
    for i in range(rows_b):
        for c in range(cols):
            pick(i, c).wait()
    for copy in copies:
        copy.wait()


def local(gradient, first_moment, second_moment, left_basis, right_basis, left_gram, right_gram, owner_slot):
    rows_b, sub_rows, width = gradient.shape
    slots_dev, size, _ = first_moment.shape
    devices = lax.axis_size("fsdp")
    cols = width // size
    state = jax.ShapeDtypeStruct(first_moment.shape, f32)
    hbm = pl.BlockSpec(memory_space=pltpu.HBM)
    vmem = pl.BlockSpec(memory_space=pltpu.VMEM)
    pieces = pltpu.VMEM((slots_dev, devices, sub_rows, size), f32)
    whole = pltpu.VMEM(first_moment.shape, f32)
    pair = pltpu.VMEM((2, size, size), bf16)
    pairs = pltpu.VMEM((slots_dev, 2, size, size), bf16)
    n = len(STEPS)
    dma = pltpu.SemaphoreType.DMA
    results = pl.pallas_call(
        kernel,
        out_shape=(pltpu.VMEM((devices * slots_dev, sub_rows, size), f32),) + (whole,) * 4,
        in_specs=[hbm] * 8,
        out_specs=(vmem,) * 5,
        scratch_shapes=[
            pltpu.VMEM((rows_b * cols + 1, sub_rows, size), f32), pieces, pieces, pieces,
            pltpu.VMEM((rows_b, cols), jnp.int32), pltpu.VMEM((8, 128), jnp.int32), pltpu.SMEM((8, 128), jnp.int32),
            whole, whole,
            pairs, pairs, pairs, pairs,
            pair, pair, pair, pair, pltpu.VMEM((size, size), f32),
            pltpu.VMEM((4, 8, 128), f32), pltpu.VMEM((devices, 8, 128), f32),
            pltpu.VMEM((2, 8, 128), f32), pltpu.VMEM((8, size), f32),
            dma((cols,)), dma((2,)), dma((6,)), dma((3,)), dma((3,)), dma((n,)), dma((n,)),
            dma((2, n)), dma((2, n)), dma((2, n + 1)), dma((2, n + 1)),
        ],
        compiler_params=pltpu.CompilerParams(
            collective_id=0, has_side_effects=True, vmem_limit_bytes=52 * 1024 * 1024
        ),
    )(owner_slot, gradient, first_moment, second_moment, left_basis, right_basis, left_gram, right_gram)
    return pl.pallas_call(
        store,
        out_shape=(jax.ShapeDtypeStruct(gradient.shape, f32), state, state, state, state),
        in_specs=[hbm] + [vmem] * 5,
        out_specs=(hbm,) * 5,
        scratch_shapes=[pltpu.SMEM((rows_b, cols), jnp.int32), dma((1,)), dma((4,)), dma((rows_b, cols))],
        compiler_params=pltpu.CompilerParams(vmem_limit_bytes=16 * 1024 * 1024),
    )(owner_slot, *results)


def solution(mesh):
    in_specs = (
        P(None, "fsdp", "tp"),
        P("fsdp", None, "tp"),
        P("fsdp", None, "tp"),
        P("fsdp", None, "tp"),
        P("fsdp", None, "tp"),
        P("fsdp", None, "tp"),
        P("fsdp", None, "tp"),
        P(None, "tp"),
    )
    out_specs = (
        P(None, "fsdp", "tp"),
        P("fsdp", None, "tp"),
        P("fsdp", None, "tp"),
        P("fsdp", None, "tp"),
        P("fsdp", None, "tp"),
    )
    return jax.shard_map(local, mesh=mesh, in_specs=in_specs, out_specs=out_specs, check_vma=False)
```

```python
import functools
import math

import jax
import jax.numpy as jnp
from jax import lax
from jax.experimental import pallas as pl
from jax.experimental.pallas import tpu as pltpu
from jax.sharding import PartitionSpec as P

D = 4096
FF = 14336

first_beta = 0.9
second_beta = 0.95
gram_beta = 0.95
first_fix = 1.0 / (1.0 - 0.9**10)
second_fix = 1.0 / (1.0 - 0.95**10)
eps_value = 1e-08

MESH = pl.DeviceIdType.MESH
f32 = jnp.float32
bf16 = jnp.bfloat16

CHIP_STEPS = (
    (2, 2),
    (3, 2), (2, 3), (1, 2), (2, 1),
    (0, 2), (2, 0),
    (3, 1), (1, 3), (3, 3), (1, 1),
    (0, 3), (0, 1), (3, 0), (1, 0),
)
STEPS = tuple((a, b, c) for c in (0, 1) for a, b in CHIP_STEPS) + ((0, 0, 1),)
ROW_STEPS = (2, 1, 3, 0)


def split(value):
    high = value.astype(bf16)
    return high, (value - high.astype(f32)).astype(bf16)


def put(pair, rows, value):
    high, low = split(value)
    pair[0, rows, :] = high
    pair[1, rows, :] = low


def product(left, rows, right):
    left_high, left_low = left[0, rows, :], left[1, rows, :]
    right_high, right_low = right[0], right[1]
    total = jnp.dot(left_low, right_high, preferred_element_type=f32)
    total += jnp.dot(left_high, right_low, preferred_element_type=f32)
    return total + jnp.dot(left_high, right_high, preferred_element_type=f32)


def kernel(
    owner_in, gradient, first_in, second_in, left_in, right_in, left_stat, right_stat,
    returned, first, second, left_gram, right_gram,
    grad, packed, arrived, leaving, owner, places, block_at,
    left_raw, right_raw,
    left_basis, left_turned, right_basis, right_turned,
    block, turned, partial, normal, rotated,
    column_parts, row_parts, mine, factor,
    fetch_sem, place_sem, load_sem, column_send, column_recv, norm_send, norm_recv, in_send, in_recv, out_send, out_recv,
):
    devices, cols, size = 32, owner_in.shape[1], 512
    me = lax.axis_index("fsdp")
    tp = lax.axis_index("tp")
    my_x, my_y, my_core = me // 8, (me // 2) % 4, me % 2

    def place(step):
        a, b, c = step
        return ((my_x + a) % 4) * 8 + ((my_y + b) % 4) * 2 + (my_core + c) % 2

    loads = [
        pltpu.make_async_copy(source, target, load_sem.at[i])
        for i, (source, target) in enumerate((
            (left_in, left_raw), (right_in, right_raw), (first_in, first),
            (second_in, second), (left_stat, left_gram), (right_stat, right_gram),
        ))
    ]
    rows_b = gradient.shape[0]
    blocks = rows_b * cols
    fetches = [
        pltpu.make_async_copy(
            gradient.at[:, :, pl.ds(c * size, size)], grad.at[pl.ds(c * rows_b, rows_b)], fetch_sem.at[0]
        )
        for c in range(cols)
    ]
    fetch_owner = pltpu.make_async_copy(owner_in, owner, place_sem.at[1])
    fetch_owner.start()
    for fetch in fetches:
        fetch.start()
    grad[blocks] = jnp.zeros(grad.shape[1:], f32)

    barrier = pltpu.get_barrier_semaphore()

    def greet(k, _):
        pl.semaphore_signal(barrier, inc=1, device_id={"fsdp": (me + k) % devices}, device_id_type=MESH)
        return 0

    def greet_column(k, _):
        pl.semaphore_signal(barrier, inc=1, device_id={"tp": (tp + k) % 4}, device_id_type=MESH)
        return 0

    lax.fori_loop(1, devices, greet, 0)
    lax.fori_loop(1, 4, greet_column, 0)
    fetch_owner.wait()
    slots = lax.broadcasted_iota(jnp.int32, (rows_b, 128), 1)
    row = lax.broadcasted_iota(jnp.int32, (rows_b, 128), 0)
    found = jnp.full((rows_b, 128), -1, jnp.int32)
    for c in range(cols):
        found = jnp.maximum(found, jnp.where(owner[:, c:c + 1] == slots, row + c * rows_b, -1))
    found = jnp.max(found, axis=0, keepdims=True)
    found = jnp.where(found < 0, blocks, found)
    places[...] = jnp.broadcast_to(found, places.shape)
    to_scalars = pltpu.make_async_copy(places, block_at, place_sem.at[0])
    to_scalars.start()

    total = jnp.zeros((16, size), f32)
    whole = grad.at[pl.ds(0, blocks)]
    pltpu.make_async_copy(whole, whole, fetch_sem.at[0]).wait()

    def square(i, total):
        value = grad[i]
        return total + value * value

    total = lax.fori_loop(0, blocks, square, total, unroll=8)
    for load in loads:
        load.start()
    total = total[:8] + total[8:]
    total = total[:, 0:128] + total[:, 128:256] + total[:, 256:384] + total[:, 384:512]
    mine[0] = total
    column_parts[tp] = total
    to_scalars.wait()

    def pack(s, to):
        packed[s, to] = grad[block_at[0, 2 * to + s]]

    pl.semaphore_wait(barrier, devices - 1 + 3)

    def wait_all(view, send, recv):
        pltpu.make_async_remote_copy(
            src_ref=view, dst_ref=view, send_sem=send, recv_sem=recv,
            device_id={"fsdp": place((0, 0, 1))}, device_id_type=MESH,
        ).wait()

    def column_copy(k):
        return pltpu.make_async_remote_copy(
            src_ref=mine.at[0], dst_ref=column_parts.at[tp],
            send_sem=column_send.at[0], recv_sem=column_recv.at[0],
            device_id={"tp": (tp + k + 1) % 4}, device_id_type=MESH,
        )

    def in_copy(s, k):
        to = place(STEPS[k])
        return pltpu.make_async_remote_copy(
            src_ref=packed.at[s, to], dst_ref=arrived.at[s, me],
            send_sem=in_send.at[s], recv_sem=in_recv.at[s],
            device_id={"fsdp": to}, device_id_type=MESH,
        )

    def norm_copy(k):
        return pltpu.make_async_remote_copy(
            src_ref=mine.at[1], dst_ref=row_parts.at[me],
            send_sem=norm_send.at[0], recv_sem=norm_recv.at[0],
            device_id={"fsdp": place(STEPS[k])}, device_id_type=MESH,
        )

    def out_copy(s, a, b, c):
        to = ((my_x + a) % 4) * 8 + ((my_y + b) % 4) * 2 + (my_core + c) % 2
        return pltpu.make_async_remote_copy(
            src_ref=leaving.at[s, to], dst_ref=returned.at[2 * me + s],
            send_sem=out_send.at[s], recv_sem=out_recv.at[s],
            device_id={"fsdp": to}, device_id_type=MESH,
        )

    for k in range(3):
        column_copy(k).start()
    for k in range(len(STEPS)):
        pack(0, place(STEPS[k]))
        in_copy(0, k).start()
    wait_all(column_parts.at[pl.ds(0, 3)], column_send.at[0], column_recv.at[0])
    own = column_parts[0] + column_parts[1] + column_parts[2] + column_parts[3]
    mine[1] = own
    row_parts[me] = own
    for k in range(len(STEPS)):
        norm_copy(k).start()
    for k in range(len(STEPS)):
        pack(1, place(STEPS[k]))
        in_copy(1, k).start()
    for s in (0, 1):
        arrived[s, me] = grad[block_at[0, 2 * me + s]]

    loads[0].wait()
    loads[1].wait()

    def prepare(s, _):
        rows = pl.ds(0, size)
        left = left_raw[s]
        put(left_basis.at[s], rows, left)
        put(left_turned.at[s], rows, left.T)
        right = right_raw[s]
        put(right_basis.at[s], rows, right)
        put(right_turned.at[s], rows, right.T)
        return 0

    lax.fori_loop(0, 2, prepare, 0)
    for load in loads[2:]:
        load.wait()

    def piece(s, t):
        return arrived[s, pl.ds(t * 16, 16)].reshape(256, size)

    def rotate(s):
        wait_all(arrived.at[s, pl.ds(0, devices - 1)], in_send.at[s], in_recv.at[s])
        for t in range(2):
            put(block, pl.ds(t * 256, 256), piece(s, t))

        def to_partial(t, _):
            rows = pl.ds(pl.multiple_of(t * 256, 256), 256)
            put(partial, rows, product(left_turned.at[s], rows, block))
            return 0

        lax.fori_loop(0, 2, to_partial, 0)

        def to_rotated(t, _):
            rows = pl.ds(pl.multiple_of(t * 256, 256), 256)
            rotated[rows, :] = product(partial, rows, right_basis.at[s])
            return 0

        lax.fori_loop(0, 2, to_rotated, 0)

    def finish_norm():
        wait_all(row_parts.at[pl.ds(0, devices - 1)], norm_send.at[0], norm_recv.at[0])
        parts = row_parts[0]
        for d in range(1, devices):
            parts = parts + row_parts[d]
        norm_sq = jnp.sum(jnp.sum(parts, axis=0, keepdims=True), axis=1, keepdims=True)
        scale = jnp.minimum(1.0, math.sqrt(D * FF) / jnp.sqrt(norm_sq))
        factor[...] = jnp.broadcast_to(scale, factor.shape)

    def rest(s):
        def update(t, _):
            rows = pl.ds(pl.multiple_of(t * 64, 64), 64)
            turn = rotated[rows, :] * factor[0:1, :]
            first_next = first_beta * first[s, rows, :] + (1.0 - first_beta) * turn
            second_next = second_beta * second[s, rows, :] + (1.0 - second_beta) * turn * turn
            first[s, rows, :] = first_next
            second[s, rows, :] = second_next
            put(normal, rows, first_fix * first_next / (jnp.sqrt(second_fix * second_next) + eps_value))
            return 0

        lax.fori_loop(0, size // 64, update, 0)

        def to_partial(t, _):
            rows = pl.ds(pl.multiple_of(t * 256, 256), 256)
            put(partial, rows, product(left_basis.at[s], rows, normal))
            return 0

        lax.fori_loop(0, 2, to_partial, 0)

        for a in ROW_STEPS:
            to_x = (my_x + a) % 4
            rows = pl.ds(pl.multiple_of(to_x * 128, 128), 128)
            leaving[s, pl.ds(to_x * 8, 8)] = product(partial, rows, right_turned.at[s]).reshape(8, 16, size)
            for c in (0, 1):
                for b in ROW_STEPS:
                    if (a, b, c) != (0, 0, 0):
                        out_copy(s, a, b, c).start()
        returned[2 * me + s] = leaving[s, me]

    rotate(0)
    finish_norm()
    rest(0)
    rotate(1)
    rest(1)

    gram_scale = factor[0:1, :] * factor[0:1, :] * ((1.0 - gram_beta) / size)
    def grams(s, _):
        def load(t, _):
            rows = pl.ds(pl.multiple_of(t * 256, 256), 256)
            put(block, rows, piece(s, t))
            return 0

        lax.fori_loop(0, 2, load, 0)
        put(turned, pl.ds(0, size), arrived[s].reshape(size, size).T)

        def step(t, _):
            rows = pl.ds(pl.multiple_of(t * 256, 256), 256)
            left_gram[s, rows, :] = gram_beta * left_gram[s, rows, :] + gram_scale * product(block, rows, turned)
            right_gram[s, rows, :] = gram_beta * right_gram[s, rows, :] + gram_scale * product(turned, rows, block)
            return 0

        lax.fori_loop(0, 2, step, 0)
        return 0

    lax.fori_loop(0, 2, grams, 0)

    for s in (0, 1):
        wait_all(returned.at[pl.ds(0, devices - 1)], out_send.at[s], out_recv.at[s])


def store(
    owner_in, returned, first, second, left_gram, right_gram,
    direction, first_out, second_out, left_out, right_out,
    owner, owner_sem, sem, block_sem,
):
    rows_b, cols = owner_in.shape
    size = returned.shape[2]
    copies = [
        pltpu.make_async_copy(source, target, sem.at[i])
        for i, (source, target) in enumerate(
            ((first, first_out), (second, second_out), (left_gram, left_out), (right_gram, right_out))
        )
    ]

    def pick(i, c):
        return pltpu.make_async_copy(
            returned.at[owner[i, c]], direction.at[i, :, pl.ds(c * size, size)], block_sem.at[0]
        )

    fetch_owner = pltpu.make_async_copy(owner_in, owner, owner_sem.at[0])
    fetch_owner.start()
    for copy in copies:
        copy.start()
    fetch_owner.wait()
    for i in range(rows_b):
        for c in range(cols):
            pick(i, c).start()
    pltpu.make_async_copy(direction, direction, block_sem.at[0]).wait()
    for copy in copies:
        copy.wait()


def local(gradient, first_moment, second_moment, left_basis, right_basis, left_gram, right_gram, owner_slot):
    rows_b, sub_rows, width = gradient.shape
    slots_dev, size, _ = first_moment.shape
    devices = lax.axis_size("fsdp")
    cols = width // size
    state = jax.ShapeDtypeStruct(first_moment.shape, f32)
    hbm = pl.BlockSpec(memory_space=pltpu.HBM)
    vmem = pl.BlockSpec(memory_space=pltpu.VMEM)
    pieces = pltpu.VMEM((slots_dev, devices, sub_rows, size), f32)
    whole = pltpu.VMEM(first_moment.shape, f32)
    pair = pltpu.VMEM((2, size, size), bf16)
    pairs = pltpu.VMEM((slots_dev, 2, size, size), bf16)
    dma = pltpu.SemaphoreType.DMA
    results = pl.pallas_call(
        kernel,
        out_shape=(pltpu.VMEM((devices * slots_dev, sub_rows, size), f32),) + (whole,) * 4,
        in_specs=[hbm] * 8,
        out_specs=(vmem,) * 5,
        scratch_shapes=[
            pltpu.VMEM((rows_b * cols + 1, sub_rows, size), f32), pieces, pieces, pieces,
            pltpu.VMEM((rows_b, cols), jnp.int32), pltpu.VMEM((8, 128), jnp.int32), pltpu.SMEM((8, 128), jnp.int32),
            whole, whole,
            pairs, pairs, pairs, pairs,
            pair, pair, pair, pair, pltpu.VMEM((size, size), f32),
            pltpu.VMEM((4, 8, 128), f32), pltpu.VMEM((devices, 8, 128), f32),
            pltpu.VMEM((2, 8, 128), f32), pltpu.VMEM((8, size), f32),
            dma((1,)), dma((2,)), dma((6,)), dma((1,)), dma((1,)), dma((1,)), dma((1,)),
            dma((2,)), dma((2,)), dma((2,)), dma((2,)),
        ],
        compiler_params=pltpu.CompilerParams(
            collective_id=0, has_side_effects=True, vmem_limit_bytes=52 * 1024 * 1024
        ),
    )(owner_slot, gradient, first_moment, second_moment, left_basis, right_basis, left_gram, right_gram)
    return pl.pallas_call(
        store,
        out_shape=(jax.ShapeDtypeStruct(gradient.shape, f32), state, state, state, state),
        in_specs=[hbm] + [vmem] * 5,
        out_specs=(hbm,) * 5,
        scratch_shapes=[pltpu.SMEM((rows_b, cols), jnp.int32), dma((1,)), dma((4,)), dma((1,))],
        compiler_params=pltpu.CompilerParams(vmem_limit_bytes=16 * 1024 * 1024),
    )(owner_slot, *results)


def solution(mesh):
    in_specs = (
        P(None, "fsdp", "tp"),
        P("fsdp", None, "tp"),
        P("fsdp", None, "tp"),
        P("fsdp", None, "tp"),
        P("fsdp", None, "tp"),
        P("fsdp", None, "tp"),
        P("fsdp", None, "tp"),
        P(None, "tp"),
    )
    out_specs = (
        P(None, "fsdp", "tp"),
        P("fsdp", None, "tp"),
        P("fsdp", None, "tp"),
        P("fsdp", None, "tp"),
        P("fsdp", None, "tp"),
    )
    return jax.shard_map(local, mesh=mesh, in_specs=in_specs, out_specs=out_specs, check_vma=False)
```

```python
import functools
import math

import jax
import jax.numpy as jnp
from jax import lax
from jax.experimental import pallas as pl
from jax.experimental.pallas import tpu as pltpu
from jax.sharding import PartitionSpec as P

D = 4096
FF = 14336

first_beta = 0.9
second_beta = 0.95
gram_beta = 0.95
first_fix = 1.0 / (1.0 - 0.9**10)
second_fix = 1.0 / (1.0 - 0.95**10)
eps_value = 1e-08

MESH = pl.DeviceIdType.MESH
f32 = jnp.float32
bf16 = jnp.bfloat16

CHIP_STEPS = (
    (2, 2),
    (3, 2), (2, 3), (1, 2), (2, 1),
    (0, 2), (2, 0),
    (3, 1), (1, 3), (3, 3), (1, 1),
    (0, 3), (0, 1), (3, 0), (1, 0),
)
STEPS = tuple((a, b, c) for c in (0, 1) for a, b in CHIP_STEPS) + ((0, 0, 1),)
ROW_STEPS = (2, 1, 3, 0)


def split(value):
    high = value.astype(bf16)
    return high, (value - high.astype(f32)).astype(bf16)


def put(pair, rows, value):
    high, low = split(value)
    pair[0, rows, :] = high
    pair[1, rows, :] = low


def product(left, rows, right):
    left_high, left_low = left[0, rows, :], left[1, rows, :]
    right_high, right_low = right[0], right[1]
    total = jnp.dot(left_low, right_high, preferred_element_type=f32)
    total += jnp.dot(left_high, right_low, preferred_element_type=f32)
    return total + jnp.dot(left_high, right_high, preferred_element_type=f32)


def kernel(
    owner_in, gradient, first_in, second_in, left_in, right_in, left_stat, right_stat,
    returned, first, second, left_gram, right_gram,
    grad, packed, arrived, leaving, owner, places, block_at,
    left_raw, right_raw,
    left_basis, left_turned, right_basis, right_turned,
    block, turned, partial, normal, rotated,
    column_parts, row_parts, mine, factor,
    fetch_sem, place_sem, load_sem, column_send, column_recv, norm_send, norm_recv, in_send, in_recv, out_send, out_recv,
):
    devices, cols, size = 32, owner_in.shape[1], 512
    me = lax.axis_index("fsdp")
    tp = lax.axis_index("tp")
    my_x, my_y, my_core = me // 8, (me // 2) % 4, me % 2

    def place(step):
        a, b, c = step
        return ((my_x + a) % 4) * 8 + ((my_y + b) % 4) * 2 + (my_core + c) % 2

    loads = [
        pltpu.make_async_copy(source, target, load_sem.at[i])
        for i, (source, target) in enumerate((
            (left_in, left_raw), (right_in, right_raw), (first_in, first),
            (second_in, second), (left_stat, left_gram), (right_stat, right_gram),
        ))
    ]
    rows_b = gradient.shape[0]
    blocks = rows_b * cols
    fetches = [
        pltpu.make_async_copy(
            gradient.at[:, :, pl.ds(c * size, size)], grad.at[pl.ds(c * rows_b, rows_b)], fetch_sem.at[0]
        )
        for c in range(cols)
    ]
    fetch_owner = pltpu.make_async_copy(owner_in, owner, place_sem.at[1])
    fetch_owner.start()
    for fetch in fetches:
        fetch.start()
    grad[blocks] = jnp.zeros(grad.shape[1:], f32)

    barrier = pltpu.get_barrier_semaphore()

    def greet_column(k, _):
        pl.semaphore_signal(barrier, inc=1, device_id={"tp": (tp + k) % 4}, device_id_type=MESH)
        return 0

    for step in STEPS:
        pl.semaphore_signal(barrier, inc=1, device_id={"fsdp": place(step)}, device_id_type=MESH)
    lax.fori_loop(1, 4, greet_column, 0)
    fetch_owner.wait()
    slots = lax.broadcasted_iota(jnp.int32, (rows_b, 128), 1)
    row = lax.broadcasted_iota(jnp.int32, (rows_b, 128), 0)
    found = jnp.full((rows_b, 128), -1, jnp.int32)
    for c in range(cols):
        found = jnp.maximum(found, jnp.where(owner[:, c:c + 1] == slots, row + c * rows_b, -1))
    found = jnp.max(found, axis=0, keepdims=True)
    found = jnp.where(found < 0, blocks, found)
    places[...] = jnp.broadcast_to(found, places.shape)
    to_scalars = pltpu.make_async_copy(places, block_at, place_sem.at[0])
    to_scalars.start()

    total = jnp.zeros((16, size), f32)
    whole = grad.at[pl.ds(0, blocks)]
    pltpu.make_async_copy(whole, whole, fetch_sem.at[0]).wait()

    def square(i, total):
        value = grad[i]
        return total + value * value

    total = lax.fori_loop(0, blocks, square, total, unroll=8)
    for load in loads:
        load.start()
    total = jnp.sum(total, axis=0, keepdims=True)
    total = total[:, 0:128] + total[:, 128:256] + total[:, 256:384] + total[:, 384:512]
    mine[0] = total
    column_parts[tp] = total
    to_scalars.wait()

    def pack(s, to):
        packed[s, to] = grad[block_at[0, 2 * to + s]]

    pl.semaphore_wait(barrier, devices - 1 + 3)

    def wait_all(view, send, recv):
        pltpu.make_async_remote_copy(
            src_ref=view, dst_ref=view, send_sem=send, recv_sem=recv,
            device_id={"fsdp": place((0, 0, 1))}, device_id_type=MESH,
        ).wait()

    def column_copy(k):
        return pltpu.make_async_remote_copy(
            src_ref=mine.at[0], dst_ref=column_parts.at[tp],
            send_sem=column_send.at[0], recv_sem=column_recv.at[0],
            device_id={"tp": (tp + k + 1) % 4}, device_id_type=MESH,
        )

    def in_copy(s, k):
        to = place(STEPS[k])
        return pltpu.make_async_remote_copy(
            src_ref=packed.at[s, to], dst_ref=arrived.at[s, me],
            send_sem=in_send.at[s], recv_sem=in_recv.at[s],
            device_id={"fsdp": to}, device_id_type=MESH,
        )

    def norm_copy(k):
        return pltpu.make_async_remote_copy(
            src_ref=mine.at[1], dst_ref=row_parts.at[me],
            send_sem=norm_send.at[0], recv_sem=norm_recv.at[0],
            device_id={"fsdp": place(STEPS[k])}, device_id_type=MESH,
        )

    def out_copy(s, a, b, c):
        to = ((my_x + a) % 4) * 8 + ((my_y + b) % 4) * 2 + (my_core + c) % 2
        return pltpu.make_async_remote_copy(
            src_ref=leaving.at[s, to], dst_ref=returned.at[2 * me + s],
            send_sem=out_send.at[s], recv_sem=out_recv.at[s],
            device_id={"fsdp": to}, device_id_type=MESH,
        )

    for k in range(3):
        column_copy(k).start()
    for k in range(len(STEPS)):
        pack(0, place(STEPS[k]))
        in_copy(0, k).start()
    wait_all(column_parts.at[pl.ds(0, 3)], column_send.at[0], column_recv.at[0])
    own = column_parts[0] + column_parts[1] + column_parts[2] + column_parts[3]
    mine[1] = own
    row_parts[me] = own
    for k in range(len(STEPS)):
        norm_copy(k).start()
    for k in range(len(STEPS)):
        pack(1, place(STEPS[k]))
        in_copy(1, k).start()
    for s in (0, 1):
        arrived[s, me] = grad[block_at[0, 2 * me + s]]

    loads[0].wait()
    loads[1].wait()

    def prepare(s, _):
        rows = pl.ds(0, size)
        left = left_raw[s]
        put(left_basis.at[s], rows, left)
        put(left_turned.at[s], rows, left.T)
        right = right_raw[s]
        put(right_basis.at[s], rows, right)
        put(right_turned.at[s], rows, right.T)
        return 0

    lax.fori_loop(0, 2, prepare, 0)
    for load in loads[2:]:
        load.wait()

    def piece(s, t):
        return arrived[s, pl.ds(t * 16, 16)].reshape(256, size)

    def rotate(s):
        wait_all(arrived.at[s, pl.ds(0, devices - 1)], in_send.at[s], in_recv.at[s])
        for t in range(2):
            put(block, pl.ds(t * 256, 256), piece(s, t))

        def to_partial(t, _):
            rows = pl.ds(pl.multiple_of(t * 256, 256), 256)
            put(partial, rows, product(left_turned.at[s], rows, block))
            return 0

        lax.fori_loop(0, 2, to_partial, 0)

        def to_rotated(t, _):
            rows = pl.ds(pl.multiple_of(t * 256, 256), 256)
            rotated[rows, :] = product(partial, rows, right_basis.at[s])
            return 0

        lax.fori_loop(0, 2, to_rotated, 0)

    def finish_norm():
        wait_all(row_parts.at[pl.ds(0, devices - 1)], norm_send.at[0], norm_recv.at[0])
        norm_sq = jnp.sum(jnp.sum(row_parts[...], axis=0), axis=1, keepdims=True)
        scale = jnp.minimum(1.0, math.sqrt(D * FF) / jnp.sqrt(norm_sq))
        factor[...] = jnp.broadcast_to(scale, factor.shape)

    def rest(s):
        def update(t, _):
            rows = pl.ds(pl.multiple_of(t * 64, 64), 64)
            turn = rotated[rows, :] * factor[0:1, :]
            first_next = first_beta * first[s, rows, :] + (1.0 - first_beta) * turn
            second_next = second_beta * second[s, rows, :] + (1.0 - second_beta) * turn * turn
            first[s, rows, :] = first_next
            second[s, rows, :] = second_next
            put(normal, rows, first_fix * first_next / (jnp.sqrt(second_fix * second_next) + eps_value))
            return 0

        lax.fori_loop(0, size // 64, update, 0)

        def to_partial(t, _):
            rows = pl.ds(pl.multiple_of(t * 256, 256), 256)
            put(partial, rows, product(left_basis.at[s], rows, normal))
            return 0

        lax.fori_loop(0, 2, to_partial, 0)

        for a in ROW_STEPS:
            to_x = (my_x + a) % 4
            rows = pl.ds(pl.multiple_of(to_x * 128, 128), 128)
            leaving[s, pl.ds(to_x * 8, 8)] = product(partial, rows, right_turned.at[s]).reshape(8, 16, size)
            for c in (0, 1):
                for b in ROW_STEPS:
                    if (a, b, c) != (0, 0, 0):
                        out_copy(s, a, b, c).start()
        returned[2 * me + s] = leaving[s, me]

    rotate(0)
    finish_norm()
    rest(0)
    rotate(1)
    rest(1)

    gram_scale = factor[0:1, :] * factor[0:1, :] * ((1.0 - gram_beta) / size)
    def grams(s, _):
        def load(t, _):
            rows = pl.ds(pl.multiple_of(t * 256, 256), 256)
            put(block, rows, piece(s, t))
            return 0

        lax.fori_loop(0, 2, load, 0)
        put(turned, pl.ds(0, size), arrived[s].reshape(size, size).T)

        def step(t, _):
            rows = pl.ds(pl.multiple_of(t * 256, 256), 256)
            left_gram[s, rows, :] = gram_beta * left_gram[s, rows, :] + gram_scale * product(block, rows, turned)
            right_gram[s, rows, :] = gram_beta * right_gram[s, rows, :] + gram_scale * product(turned, rows, block)
            return 0

        lax.fori_loop(0, 2, step, 0)
        return 0

    lax.fori_loop(0, 2, grams, 0)

    for s in (0, 1):
        wait_all(returned.at[pl.ds(0, devices - 1)], out_send.at[s], out_recv.at[s])


def store(
    owner_in, returned, first, second, left_gram, right_gram,
    direction, first_out, second_out, left_out, right_out,
    owner, owner_sem, sem, block_sem,
):
    rows_b, cols = owner_in.shape
    size = returned.shape[2]
    copies = [
        pltpu.make_async_copy(source, target, sem.at[i])
        for i, (source, target) in enumerate(
            ((first, first_out), (second, second_out), (left_gram, left_out), (right_gram, right_out))
        )
    ]

    def pick(i, c):
        return pltpu.make_async_copy(
            returned.at[owner[i, c]], direction.at[i, :, pl.ds(c * size, size)], block_sem.at[0]
        )

    fetch_owner = pltpu.make_async_copy(owner_in, owner, owner_sem.at[0])
    fetch_owner.start()
    for copy in copies:
        copy.start()
    fetch_owner.wait()
    for i in range(rows_b):
        for c in range(cols):
            pick(i, c).start()
    pltpu.make_async_copy(direction, direction, block_sem.at[0]).wait()
    for copy in copies:
        copy.wait()


def local(gradient, first_moment, second_moment, left_basis, right_basis, left_gram, right_gram, owner_slot):
    rows_b, sub_rows, width = gradient.shape
    slots_dev, size, _ = first_moment.shape
    devices = lax.axis_size("fsdp")
    cols = width // size
    state = jax.ShapeDtypeStruct(first_moment.shape, f32)
    hbm = pl.BlockSpec(memory_space=pltpu.HBM)
    vmem = pl.BlockSpec(memory_space=pltpu.VMEM)
    pieces = pltpu.VMEM((slots_dev, devices, sub_rows, size), f32)
    whole = pltpu.VMEM(first_moment.shape, f32)
    pair = pltpu.VMEM((2, size, size), bf16)
    pairs = pltpu.VMEM((slots_dev, 2, size, size), bf16)
    dma = pltpu.SemaphoreType.DMA
    results = pl.pallas_call(
        kernel,
        out_shape=(pltpu.VMEM((devices * slots_dev, sub_rows, size), f32),) + (whole,) * 4,
        in_specs=[hbm] * 8,
        out_specs=(vmem,) * 5,
        scratch_shapes=[
            pltpu.VMEM((rows_b * cols + 1, sub_rows, size), f32), pieces, pieces, pieces,
            pltpu.VMEM((rows_b, cols), jnp.int32), pltpu.VMEM((8, 128), jnp.int32), pltpu.SMEM((8, 128), jnp.int32),
            whole, whole,
            pairs, pairs, pairs, pairs,
            pair, pair, pair, pair, pltpu.VMEM((size, size), f32),
            pltpu.VMEM((4, 1, 128), f32), pltpu.VMEM((devices, 1, 128), f32),
            pltpu.VMEM((2, 1, 128), f32), pltpu.VMEM((8, size), f32),
            dma((1,)), dma((2,)), dma((6,)), dma((1,)), dma((1,)), dma((1,)), dma((1,)),
            dma((2,)), dma((2,)), dma((2,)), dma((2,)),
        ],
        compiler_params=pltpu.CompilerParams(
            collective_id=0, has_side_effects=True, vmem_limit_bytes=52 * 1024 * 1024
        ),
    )(owner_slot, gradient, first_moment, second_moment, left_basis, right_basis, left_gram, right_gram)
    return pl.pallas_call(
        store,
        out_shape=(jax.ShapeDtypeStruct(gradient.shape, f32), state, state, state, state),
        in_specs=[hbm] + [vmem] * 5,
        out_specs=(hbm,) * 5,
        scratch_shapes=[pltpu.SMEM((rows_b, cols), jnp.int32), dma((1,)), dma((4,)), dma((1,))],
        compiler_params=pltpu.CompilerParams(vmem_limit_bytes=16 * 1024 * 1024),
    )(owner_slot, *results)


def solution(mesh):
    in_specs = (
        P(None, "fsdp", "tp"),
        P("fsdp", None, "tp"),
        P("fsdp", None, "tp"),
        P("fsdp", None, "tp"),
        P("fsdp", None, "tp"),
        P("fsdp", None, "tp"),
        P("fsdp", None, "tp"),
        P(None, "tp"),
    )
    out_specs = (
        P(None, "fsdp", "tp"),
        P("fsdp", None, "tp"),
        P("fsdp", None, "tp"),
        P("fsdp", None, "tp"),
        P("fsdp", None, "tp"),
    )
    return jax.shard_map(local, mesh=mesh, in_specs=in_specs, out_specs=out_specs, check_vma=False)
```

```python
import functools
import math

import jax
import jax.numpy as jnp
from jax import lax
from jax.experimental import pallas as pl
from jax.experimental.pallas import tpu as pltpu
from jax.sharding import PartitionSpec as P

D = 4096
FF = 14336

first_beta = 0.9
second_beta = 0.95
gram_beta = 0.95
first_fix = 1.0 / (1.0 - 0.9**10)
second_fix = 1.0 / (1.0 - 0.95**10)
eps_value = 1e-08

MESH = pl.DeviceIdType.MESH
f32 = jnp.float32
bf16 = jnp.bfloat16

CHIP_STEPS = (
    (2, 2),
    (3, 2), (2, 3), (1, 2), (2, 1),
    (0, 2), (2, 0),
    (3, 1), (1, 3), (3, 3), (1, 1),
    (0, 3), (0, 1), (3, 0), (1, 0),
)
STEPS = tuple((a, b, c) for c in (0, 1) for a, b in CHIP_STEPS) + ((0, 0, 1),)
ROW_STEPS = (2, 1, 3, 0)
FIRST = 22


def split(value):
    high = value.astype(bf16)
    return high, (value - high.astype(f32)).astype(bf16)


def put(pair, rows, value):
    high, low = split(value)
    pair[0, rows, :] = high
    pair[1, rows, :] = low


def product(left, rows, right):
    left_high, left_low = left[0, rows, :], left[1, rows, :]
    right_high, right_low = right[0], right[1]
    total = jnp.dot(left_low, right_high, preferred_element_type=f32)
    total += jnp.dot(left_high, right_low, preferred_element_type=f32)
    return total + jnp.dot(left_high, right_high, preferred_element_type=f32)


def kernel(
    owner_in, gradient, first_in, second_in, left_in, right_in, left_stat, right_stat,
    returned, first, second, left_gram, right_gram,
    grad, packed, arrived, leaving, owner, places, block_at,
    left_raw, right_raw,
    left_basis, left_turned, right_basis, right_turned,
    block, turned, partial, normal, rotated,
    column_parts, row_parts, mine, norm, factor,
    fetch_sem, place_sem, load_sem, column_send, column_recv, norm_send, norm_recv, in_send, in_recv, out_send, out_recv,
):
    devices, cols, size = 32, owner_in.shape[1], 512
    me = lax.axis_index("fsdp")
    tp = lax.axis_index("tp")
    gathers = me == 0
    my_x, my_y, my_core = me // 8, (me // 2) % 4, me % 2

    def place(step):
        a, b, c = step
        return ((my_x + a) % 4) * 8 + ((my_y + b) % 4) * 2 + (my_core + c) % 2

    loads = [
        pltpu.make_async_copy(source, target, load_sem.at[i])
        for i, (source, target) in enumerate((
            (left_in, left_raw), (right_in, right_raw), (first_in, first),
            (second_in, second), (left_stat, left_gram), (right_stat, right_gram),
        ))
    ]
    rows_b = gradient.shape[0]
    blocks = rows_b * cols
    fetches = [
        pltpu.make_async_copy(
            gradient.at[:, :, pl.ds(c * size, size)], grad.at[pl.ds(c * rows_b, rows_b)], fetch_sem.at[0]
        )
        for c in range(cols)
    ]
    fetch_owner = pltpu.make_async_copy(owner_in, owner, place_sem.at[1])
    fetch_owner.start()
    for fetch in fetches:
        fetch.start()
    grad[blocks] = jnp.zeros(grad.shape[1:], f32)

    barrier = pltpu.get_barrier_semaphore()

    def greet_column(k, _):
        pl.semaphore_signal(barrier, inc=1, device_id={"tp": (tp + k) % 4}, device_id_type=MESH)
        return 0

    for step in STEPS:
        pl.semaphore_signal(barrier, inc=1, device_id={"fsdp": place(step)}, device_id_type=MESH)

    @pl.when(gathers)
    def _():
        lax.fori_loop(1, 4, greet_column, 0)

    fetch_owner.wait()
    slots = lax.broadcasted_iota(jnp.int32, (rows_b, 128), 1)
    row = lax.broadcasted_iota(jnp.int32, (rows_b, 128), 0)
    found = jnp.full((rows_b, 128), -1, jnp.int32)
    for c in range(cols):
        found = jnp.maximum(found, jnp.where(owner[:, c:c + 1] == slots, row + c * rows_b, -1))
    found = jnp.max(found, axis=0, keepdims=True)
    found = jnp.where(found < 0, blocks, found)
    places[...] = jnp.broadcast_to(found, places.shape)
    to_scalars = pltpu.make_async_copy(places, block_at, place_sem.at[0])
    to_scalars.start()

    total = jnp.zeros((16, size), f32)
    whole = grad.at[pl.ds(0, blocks)]
    pltpu.make_async_copy(whole, whole, fetch_sem.at[0]).wait()

    def square(i, total):
        value = grad[i]
        return total + value * value

    total = lax.fori_loop(0, blocks, square, total, unroll=8)
    for load in loads:
        load.start()
    total = jnp.sum(total, axis=0, keepdims=True)
    total = total[:, 0:128] + total[:, 128:256] + total[:, 256:384] + total[:, 384:512]
    mine[...] = total
    row_parts[me] = total
    to_scalars.wait()

    def pack(s, to):
        packed[s, to] = grad[block_at[0, 2 * to + s]]

    @pl.when(gathers)
    def _():
        pl.semaphore_wait(barrier, devices - 1 + 3)

    @pl.when(jnp.logical_not(gathers))
    def _():
        pl.semaphore_wait(barrier, devices - 1)

    def wait_all(view, send, recv):
        pltpu.make_async_remote_copy(
            src_ref=view, dst_ref=view, send_sem=send, recv_sem=recv,
            device_id={"fsdp": place((0, 0, 1))}, device_id_type=MESH,
        ).wait()

    def column_copy(k):
        return pltpu.make_async_remote_copy(
            src_ref=mine, dst_ref=column_parts.at[tp],
            send_sem=column_send.at[0], recv_sem=column_recv.at[0],
            device_id={"tp": (tp + k + 1) % 4}, device_id_type=MESH,
        )

    def in_copy(s, k):
        to = place(STEPS[k])
        return pltpu.make_async_remote_copy(
            src_ref=packed.at[s, to], dst_ref=arrived.at[s, me],
            send_sem=in_send.at[s], recv_sem=in_recv.at[s],
            device_id={"fsdp": to}, device_id_type=MESH,
        )

    def part_copy():
        return pltpu.make_async_remote_copy(
            src_ref=mine, dst_ref=row_parts.at[me],
            send_sem=norm_send.at[0], recv_sem=norm_recv.at[0],
            device_id={"fsdp": 0}, device_id_type=MESH,
        )

    def norm_copy(step):
        return pltpu.make_async_remote_copy(
            src_ref=norm, dst_ref=norm,
            send_sem=norm_send.at[1], recv_sem=norm_recv.at[1],
            device_id={"fsdp": place(step)}, device_id_type=MESH,
        )

    def out_copy(s, a, b, c):
        to = ((my_x + a) % 4) * 8 + ((my_y + b) % 4) * 2 + (my_core + c) % 2
        return pltpu.make_async_remote_copy(
            src_ref=leaving.at[s, to], dst_ref=returned.at[2 * me + s],
            send_sem=out_send.at[s], recv_sem=out_recv.at[s],
            device_id={"fsdp": to}, device_id_type=MESH,
        )

    @pl.when(jnp.logical_not(gathers))
    def _():
        part_copy().start()

    for k in range(FIRST):
        pack(0, place(STEPS[k]))
        in_copy(0, k).start()

    @pl.when(gathers)
    def _():
        view = row_parts.at[pl.ds(0, devices - 1)]
        pltpu.make_async_copy(view, view, norm_recv.at[0]).wait()
        plane = jnp.sum(row_parts[...], axis=0)
        mine[...] = plane
        column_parts[tp] = plane
        for k in range(3):
            column_copy(k).start()

    for k in range(FIRST, len(STEPS)):
        pack(0, place(STEPS[k]))
        in_copy(0, k).start()

    @pl.when(gathers)
    def _():
        wait_all(column_parts.at[pl.ds(0, 3)], column_send.at[0], column_recv.at[0])
        norm[...] = column_parts[0] + column_parts[1] + column_parts[2] + column_parts[3]
        for step in STEPS:
            norm_copy(step).start()

    for k in range(len(STEPS)):
        pack(1, place(STEPS[k]))
        in_copy(1, k).start()
    for s in (0, 1):
        arrived[s, me] = grad[block_at[0, 2 * me + s]]

    loads[0].wait()
    loads[1].wait()

    def prepare(s, _):
        rows = pl.ds(0, size)
        left = left_raw[s]
        put(left_basis.at[s], rows, left)
        put(left_turned.at[s], rows, left.T)
        right = right_raw[s]
        put(right_basis.at[s], rows, right)
        put(right_turned.at[s], rows, right.T)
        return 0

    lax.fori_loop(0, 2, prepare, 0)
    for load in loads[2:]:
        load.wait()

    def piece(s, t):
        return arrived[s, pl.ds(t * 16, 16)].reshape(256, size)

    def rotate(s):
        wait_all(arrived.at[s, pl.ds(0, devices - 1)], in_send.at[s], in_recv.at[s])
        for t in range(2):
            put(block, pl.ds(t * 256, 256), piece(s, t))

        def to_partial(t, _):
            rows = pl.ds(pl.multiple_of(t * 256, 256), 256)
            put(partial, rows, product(left_turned.at[s], rows, block))
            return 0

        lax.fori_loop(0, 2, to_partial, 0)

        def to_rotated(t, _):
            rows = pl.ds(pl.multiple_of(t * 256, 256), 256)
            rotated[rows, :] = product(partial, rows, right_basis.at[s])
            return 0

        lax.fori_loop(0, 2, to_rotated, 0)

    def finish_norm():
        @pl.when(gathers)
        def _():
            view = row_parts.at[pl.ds(0, devices - 1)]
            pltpu.make_async_copy(view, view, norm_send.at[1]).wait()

        @pl.when(jnp.logical_not(gathers))
        def _():
            part_copy().wait_send()
            norm_copy(STEPS[0]).wait_recv()

        norm_sq = jnp.sum(norm[...], axis=1, keepdims=True)
        scale = jnp.minimum(1.0, math.sqrt(D * FF) / jnp.sqrt(norm_sq))
        factor[...] = jnp.broadcast_to(scale, factor.shape)

    def rest(s):
        def update(t, _):
            rows = pl.ds(pl.multiple_of(t * 64, 64), 64)
            turn = rotated[rows, :] * factor[0:1, :]
            first_next = first_beta * first[s, rows, :] + (1.0 - first_beta) * turn
            second_next = second_beta * second[s, rows, :] + (1.0 - second_beta) * turn * turn
            first[s, rows, :] = first_next
            second[s, rows, :] = second_next
            put(normal, rows, first_fix * first_next / (jnp.sqrt(second_fix * second_next) + eps_value))
            return 0

        lax.fori_loop(0, size // 64, update, 0)

        def to_partial(t, _):
            rows = pl.ds(pl.multiple_of(t * 256, 256), 256)
            put(partial, rows, product(left_basis.at[s], rows, normal))
            return 0

        lax.fori_loop(0, 2, to_partial, 0)

        for a in ROW_STEPS:
            to_x = (my_x + a) % 4
            rows = pl.ds(pl.multiple_of(to_x * 128, 128), 128)
            leaving[s, pl.ds(to_x * 8, 8)] = product(partial, rows, right_turned.at[s]).reshape(8, 16, size)
            for c in (0, 1):
                for b in ROW_STEPS:
                    if (a, b, c) != (0, 0, 0):
                        out_copy(s, a, b, c).start()
        returned[2 * me + s] = leaving[s, me]

    rotate(0)
    finish_norm()
    rest(0)
    rotate(1)
    rest(1)

    gram_scale = factor[0:1, :] * factor[0:1, :] * ((1.0 - gram_beta) / size)
    def grams(s, _):
        def load(t, _):
            rows = pl.ds(pl.multiple_of(t * 256, 256), 256)
            put(block, rows, piece(s, t))
            return 0

        lax.fori_loop(0, 2, load, 0)
        put(turned, pl.ds(0, size), arrived[s].reshape(size, size).T)

        def step(t, _):
            rows = pl.ds(pl.multiple_of(t * 256, 256), 256)
            left_gram[s, rows, :] = gram_beta * left_gram[s, rows, :] + gram_scale * product(block, rows, turned)
            right_gram[s, rows, :] = gram_beta * right_gram[s, rows, :] + gram_scale * product(turned, rows, block)
            return 0

        lax.fori_loop(0, 2, step, 0)
        return 0

    lax.fori_loop(0, 2, grams, 0)

    for s in (0, 1):
        wait_all(returned.at[pl.ds(0, devices - 1)], out_send.at[s], out_recv.at[s])


def store(
    owner_in, returned, first, second, left_gram, right_gram,
    direction, first_out, second_out, left_out, right_out,
    owner, owner_sem, sem, block_sem,
):
    rows_b, cols = owner_in.shape
    size = returned.shape[2]
    copies = [
        pltpu.make_async_copy(source, target, sem.at[i])
        for i, (source, target) in enumerate(
            ((first, first_out), (second, second_out), (left_gram, left_out), (right_gram, right_out))
        )
    ]

    def pick(i, c):
        return pltpu.make_async_copy(
            returned.at[owner[i, c]], direction.at[i, :, pl.ds(c * size, size)], block_sem.at[0]
        )

    fetch_owner = pltpu.make_async_copy(owner_in, owner, owner_sem.at[0])
    fetch_owner.start()
    for copy in copies:
        copy.start()
    fetch_owner.wait()
    for i in range(rows_b):
        for c in range(cols):
            pick(i, c).start()
    pltpu.make_async_copy(direction, direction, block_sem.at[0]).wait()
    for copy in copies:
        copy.wait()


def local(gradient, first_moment, second_moment, left_basis, right_basis, left_gram, right_gram, owner_slot):
    rows_b, sub_rows, width = gradient.shape
    slots_dev, size, _ = first_moment.shape
    devices = lax.axis_size("fsdp")
    cols = width // size
    state = jax.ShapeDtypeStruct(first_moment.shape, f32)
    hbm = pl.BlockSpec(memory_space=pltpu.HBM)
    vmem = pl.BlockSpec(memory_space=pltpu.VMEM)
    pieces = pltpu.VMEM((slots_dev, devices, sub_rows, size), f32)
    whole = pltpu.VMEM(first_moment.shape, f32)
    pair = pltpu.VMEM((2, size, size), bf16)
    pairs = pltpu.VMEM((slots_dev, 2, size, size), bf16)
    dma = pltpu.SemaphoreType.DMA
    results = pl.pallas_call(
        kernel,
        out_shape=(pltpu.VMEM((devices * slots_dev, sub_rows, size), f32),) + (whole,) * 4,
        in_specs=[hbm] * 8,
        out_specs=(vmem,) * 5,
        scratch_shapes=[
            pltpu.VMEM((rows_b * cols + 1, sub_rows, size), f32), pieces, pieces, pieces,
            pltpu.VMEM((rows_b, cols), jnp.int32), pltpu.VMEM((8, 128), jnp.int32), pltpu.SMEM((8, 128), jnp.int32),
            whole, whole,
            pairs, pairs, pairs, pairs,
            pair, pair, pair, pair, pltpu.VMEM((size, size), f32),
            pltpu.VMEM((4, 1, 128), f32), pltpu.VMEM((devices, 1, 128), f32),
            pltpu.VMEM((1, 128), f32), pltpu.VMEM((1, 128), f32), pltpu.VMEM((8, size), f32),
            dma((1,)), dma((2,)), dma((6,)), dma((1,)), dma((1,)), dma((2,)), dma((2,)),
            dma((2,)), dma((2,)), dma((2,)), dma((2,)),
        ],
        compiler_params=pltpu.CompilerParams(
            collective_id=0, has_side_effects=True, vmem_limit_bytes=52 * 1024 * 1024
        ),
    )(owner_slot, gradient, first_moment, second_moment, left_basis, right_basis, left_gram, right_gram)
    return pl.pallas_call(
        store,
        out_shape=(jax.ShapeDtypeStruct(gradient.shape, f32), state, state, state, state),
        in_specs=[hbm] + [vmem] * 5,
        out_specs=(hbm,) * 5,
        scratch_shapes=[pltpu.SMEM((rows_b, cols), jnp.int32), dma((1,)), dma((4,)), dma((1,))],
        compiler_params=pltpu.CompilerParams(vmem_limit_bytes=16 * 1024 * 1024),
    )(owner_slot, *results)


def solution(mesh):
    in_specs = (
        P(None, "fsdp", "tp"),
        P("fsdp", None, "tp"),
        P("fsdp", None, "tp"),
        P("fsdp", None, "tp"),
        P("fsdp", None, "tp"),
        P("fsdp", None, "tp"),
        P("fsdp", None, "tp"),
        P(None, "tp"),
    )
    out_specs = (
        P(None, "fsdp", "tp"),
        P("fsdp", None, "tp"),
        P("fsdp", None, "tp"),
        P("fsdp", None, "tp"),
        P("fsdp", None, "tp"),
    )
    return jax.shard_map(local, mesh=mesh, in_specs=in_specs, out_specs=out_specs, check_vma=False)
```

```python
import functools
import math

import jax
import jax.numpy as jnp
from jax import lax
from jax.experimental import pallas as pl
from jax.experimental.pallas import tpu as pltpu
from jax.sharding import PartitionSpec as P

D = 4096
FF = 14336

first_beta = 0.9
second_beta = 0.95
gram_beta = 0.95
first_fix = 1.0 / (1.0 - 0.9**10)
second_fix = 1.0 / (1.0 - 0.95**10)
eps_value = 1e-08

MESH = pl.DeviceIdType.MESH
f32 = jnp.float32
bf16 = jnp.bfloat16

CHIP_STEPS = (
    (2, 2),
    (3, 2), (2, 3), (1, 2), (2, 1),
    (0, 2), (2, 0),
    (3, 1), (1, 3), (3, 3), (1, 1),
    (0, 3), (0, 1), (3, 0), (1, 0),
)
STEPS = tuple((a, b, c) for c in (0, 1) for a, b in CHIP_STEPS) + ((0, 0, 1),)
ROW_STEPS = (2, 1, 3, 0)
FIRST = 22


def split(value):
    high = value.astype(bf16)
    return high, (value - high.astype(f32)).astype(bf16)


def put(pair, rows, value):
    high, low = split(value)
    pair[0, rows, :] = high
    pair[1, rows, :] = low


def product(left, rows, right):
    left_high, left_low = left[0, rows, :], left[1, rows, :]
    right_high, right_low = right[0], right[1]
    total = jnp.dot(left_low, right_high, preferred_element_type=f32)
    total += jnp.dot(left_high, right_low, preferred_element_type=f32)
    return total + jnp.dot(left_high, right_high, preferred_element_type=f32)


def kernel(
    owner_in, gradient, first_in, second_in, left_in, right_in, left_stat, right_stat,
    returned, first, second, left_gram, right_gram,
    grad, packed, arrived, leaving, owner, places, block_at,
    left_raw, right_raw,
    left_basis, left_turned, right_basis, right_turned,
    block, turned, partial, normal, rotated,
    column_parts, row_parts, mine, norm, factor,
    fetch_sem, place_sem, load_sem, column_send, column_recv, norm_send, norm_recv, in_send, in_recv, out_send, out_recv,
):
    devices, cols, size = 32, owner_in.shape[1], 512
    me = lax.axis_index("fsdp")
    tp = lax.axis_index("tp")
    gathers = me == 0
    my_x, my_y, my_core = me // 8, (me // 2) % 4, me % 2

    def place(step):
        a, b, c = step
        return ((my_x + a) % 4) * 8 + ((my_y + b) % 4) * 2 + (my_core + c) % 2

    barrier = pltpu.get_barrier_semaphore()

    def greet_column(k, _):
        pl.semaphore_signal(barrier, inc=1, device_id={"tp": (tp + k) % 4}, device_id_type=MESH)
        return 0

    for step in STEPS:
        pl.semaphore_signal(barrier, inc=1, device_id={"fsdp": place(step)}, device_id_type=MESH)

    @pl.when(gathers)
    def _():
        lax.fori_loop(1, 4, greet_column, 0)

    loads = [
        pltpu.make_async_copy(source, target, load_sem.at[i])
        for i, (source, target) in enumerate((
            (left_in, left_raw), (right_in, right_raw), (first_in, first),
            (second_in, second), (left_stat, left_gram), (right_stat, right_gram),
        ))
    ]
    rows_b = gradient.shape[0]
    blocks = rows_b * cols
    fetches = [
        pltpu.make_async_copy(
            gradient.at[:, :, pl.ds(c * size, size)], grad.at[pl.ds(c * rows_b, rows_b)], fetch_sem.at[0]
        )
        for c in range(cols)
    ]
    fetch_owner = pltpu.make_async_copy(owner_in, owner, place_sem.at[1])
    fetch_owner.start()
    for fetch in fetches:
        fetch.start()
    grad[blocks] = jnp.zeros(grad.shape[1:], f32)

    fetch_owner.wait()
    slots = lax.broadcasted_iota(jnp.int32, (rows_b, 128), 1)
    row = lax.broadcasted_iota(jnp.int32, (rows_b, 128), 0)
    found = jnp.full((rows_b, 128), -1, jnp.int32)
    for c in range(cols):
        found = jnp.maximum(found, jnp.where(owner[:, c:c + 1] == slots, row + c * rows_b, -1))
    found = jnp.max(found, axis=0, keepdims=True)
    found = jnp.where(found < 0, blocks, found)
    places[...] = jnp.broadcast_to(found, places.shape)
    to_scalars = pltpu.make_async_copy(places, block_at, place_sem.at[0])
    to_scalars.start()

    total = jnp.zeros((16, size), f32)
    whole = grad.at[pl.ds(0, blocks)]
    pltpu.make_async_copy(whole, whole, fetch_sem.at[0]).wait()

    def square(i, total):
        value = grad[i]
        return total + value * value

    total = lax.fori_loop(0, blocks, square, total, unroll=8)
    for load in loads:
        load.start()
    total = jnp.sum(total, axis=0, keepdims=True)
    total = total[:, 0:128] + total[:, 128:256] + total[:, 256:384] + total[:, 384:512]
    mine[...] = total
    row_parts[me] = total
    to_scalars.wait()

    def pack(s, to):
        packed[s, to] = grad[block_at[0, 2 * to + s]]

    @pl.when(gathers)
    def _():
        pl.semaphore_wait(barrier, devices - 1 + 3)

    @pl.when(jnp.logical_not(gathers))
    def _():
        pl.semaphore_wait(barrier, devices - 1)

    def wait_all(view, send, recv):
        pltpu.make_async_remote_copy(
            src_ref=view, dst_ref=view, send_sem=send, recv_sem=recv,
            device_id={"fsdp": place((0, 0, 1))}, device_id_type=MESH,
        ).wait()

    def column_copy(k):
        return pltpu.make_async_remote_copy(
            src_ref=mine, dst_ref=column_parts.at[tp],
            send_sem=column_send.at[0], recv_sem=column_recv.at[0],
            device_id={"tp": (tp + k + 1) % 4}, device_id_type=MESH,
        )

    def in_copy(s, k):
        to = place(STEPS[k])
        return pltpu.make_async_remote_copy(
            src_ref=packed.at[s, to], dst_ref=arrived.at[s, me],
            send_sem=in_send.at[s], recv_sem=in_recv.at[s],
            device_id={"fsdp": to}, device_id_type=MESH,
        )

    def part_copy():
        return pltpu.make_async_remote_copy(
            src_ref=mine, dst_ref=row_parts.at[me],
            send_sem=norm_send.at[0], recv_sem=norm_recv.at[0],
            device_id={"fsdp": 0}, device_id_type=MESH,
        )

    def norm_copy(step):
        return pltpu.make_async_remote_copy(
            src_ref=norm, dst_ref=norm,
            send_sem=norm_send.at[1], recv_sem=norm_recv.at[1],
            device_id={"fsdp": place(step)}, device_id_type=MESH,
        )

    def out_copy(s, a, b, c):
        to = ((my_x + a) % 4) * 8 + ((my_y + b) % 4) * 2 + (my_core + c) % 2
        return pltpu.make_async_remote_copy(
            src_ref=leaving.at[s, to], dst_ref=returned.at[2 * me + s],
            send_sem=out_send.at[s], recv_sem=out_recv.at[s],
            device_id={"fsdp": to}, device_id_type=MESH,
        )

    @pl.when(jnp.logical_not(gathers))
    def _():
        part_copy().start()

    for k in range(FIRST):
        pack(0, place(STEPS[k]))
        in_copy(0, k).start()

    @pl.when(gathers)
    def _():
        view = row_parts.at[pl.ds(0, devices - 1)]
        pltpu.make_async_copy(view, view, norm_recv.at[0]).wait()
        plane = jnp.sum(row_parts[...], axis=0)
        mine[...] = plane
        column_parts[tp] = plane
        for k in range(3):
            column_copy(k).start()

    for k in range(FIRST, len(STEPS)):
        pack(0, place(STEPS[k]))
        in_copy(0, k).start()

    @pl.when(gathers)
    def _():
        wait_all(column_parts.at[pl.ds(0, 3)], column_send.at[0], column_recv.at[0])
        norm[...] = column_parts[0] + column_parts[1] + column_parts[2] + column_parts[3]
        for step in STEPS:
            norm_copy(step).start()

    for k in range(len(STEPS)):
        pack(1, place(STEPS[k]))
        in_copy(1, k).start()
    for s in (0, 1):
        arrived[s, me] = grad[block_at[0, 2 * me + s]]

    loads[0].wait()
    loads[1].wait()

    def prepare(s, _):
        rows = pl.ds(0, size)
        left = left_raw[s]
        put(left_basis.at[s], rows, left)
        put(left_turned.at[s], rows, left.T)
        right = right_raw[s]
        put(right_basis.at[s], rows, right)
        put(right_turned.at[s], rows, right.T)
        return 0

    lax.fori_loop(0, 2, prepare, 0)
    for load in loads[2:]:
        load.wait()

    def piece(s, t):
        return arrived[s, pl.ds(t * 16, 16)].reshape(256, size)

    def rotate(s):
        wait_all(arrived.at[s, pl.ds(0, devices - 1)], in_send.at[s], in_recv.at[s])
        for t in range(2):
            put(block, pl.ds(t * 256, 256), piece(s, t))

        def to_partial(t, _):
            rows = pl.ds(pl.multiple_of(t * 256, 256), 256)
            put(partial, rows, product(left_turned.at[s], rows, block))
            return 0

        lax.fori_loop(0, 2, to_partial, 0)

        def to_rotated(t, _):
            rows = pl.ds(pl.multiple_of(t * 256, 256), 256)
            rotated[rows, :] = product(partial, rows, right_basis.at[s])
            return 0

        lax.fori_loop(0, 2, to_rotated, 0)

    def finish_norm():
        @pl.when(gathers)
        def _():
            view = row_parts.at[pl.ds(0, devices - 1)]
            pltpu.make_async_copy(view, view, norm_send.at[1]).wait()

        @pl.when(jnp.logical_not(gathers))
        def _():
            part_copy().wait_send()
            norm_copy(STEPS[0]).wait_recv()

        norm_sq = jnp.sum(norm[...], axis=1, keepdims=True)
        scale = jnp.minimum(1.0, math.sqrt(D * FF) / jnp.sqrt(norm_sq))
        factor[...] = jnp.broadcast_to(scale, factor.shape)

    def rest(s):
        def update(t, _):
            rows = pl.ds(pl.multiple_of(t * 64, 64), 64)
            turn = rotated[rows, :] * factor[0:1, :]
            first_next = first_beta * first[s, rows, :] + (1.0 - first_beta) * turn
            second_next = second_beta * second[s, rows, :] + (1.0 - second_beta) * turn * turn
            first[s, rows, :] = first_next
            second[s, rows, :] = second_next
            put(normal, rows, first_fix * first_next / (jnp.sqrt(second_fix * second_next) + eps_value))
            return 0

        lax.fori_loop(0, size // 64, update, 0)

        def to_partial(t, _):
            rows = pl.ds(pl.multiple_of(t * 256, 256), 256)
            put(partial, rows, product(left_basis.at[s], rows, normal))
            return 0

        lax.fori_loop(0, 2, to_partial, 0)

        for a in ROW_STEPS:
            to_x = (my_x + a) % 4
            rows = pl.ds(pl.multiple_of(to_x * 128, 128), 128)
            leaving[s, pl.ds(to_x * 8, 8)] = product(partial, rows, right_turned.at[s]).reshape(8, 16, size)
            for c in (0, 1):
                for b in ROW_STEPS:
                    if (a, b, c) != (0, 0, 0):
                        out_copy(s, a, b, c).start()
        returned[2 * me + s] = leaving[s, me]

    rotate(0)
    finish_norm()
    rest(0)
    rotate(1)
    rest(1)

    gram_scale = factor[0:1, :] * factor[0:1, :] * ((1.0 - gram_beta) / size)
    def grams(s, _):
        def load(t, _):
            rows = pl.ds(pl.multiple_of(t * 256, 256), 256)
            put(block, rows, piece(s, t))
            return 0

        lax.fori_loop(0, 2, load, 0)
        put(turned, pl.ds(0, size), arrived[s].reshape(size, size).T)

        def step(t, _):
            rows = pl.ds(pl.multiple_of(t * 256, 256), 256)
            left_gram[s, rows, :] = gram_beta * left_gram[s, rows, :] + gram_scale * product(block, rows, turned)
            right_gram[s, rows, :] = gram_beta * right_gram[s, rows, :] + gram_scale * product(turned, rows, block)
            return 0

        lax.fori_loop(0, 2, step, 0)
        return 0

    lax.fori_loop(0, 2, grams, 0)

    for s in (0, 1):
        wait_all(returned.at[pl.ds(0, devices - 1)], out_send.at[s], out_recv.at[s])


def store(
    owner_in, returned, first, second, left_gram, right_gram,
    direction, first_out, second_out, left_out, right_out,
    owner, owner_sem, sem, block_sem,
):
    rows_b, cols = owner_in.shape
    size = returned.shape[2]
    copies = [
        pltpu.make_async_copy(source, target, sem.at[i])
        for i, (source, target) in enumerate(
            ((first, first_out), (second, second_out), (left_gram, left_out), (right_gram, right_out))
        )
    ]

    def pick(i, c):
        return pltpu.make_async_copy(
            returned.at[owner[i, c]], direction.at[i, :, pl.ds(c * size, size)], block_sem.at[0]
        )

    fetch_owner = pltpu.make_async_copy(owner_in, owner, owner_sem.at[0])
    fetch_owner.start()
    for copy in copies:
        copy.start()
    fetch_owner.wait()
    for i in range(rows_b):
        for c in range(cols):
            pick(i, c).start()
    pltpu.make_async_copy(direction, direction, block_sem.at[0]).wait()
    for copy in copies:
        copy.wait()


def local(gradient, first_moment, second_moment, left_basis, right_basis, left_gram, right_gram, owner_slot):
    rows_b, sub_rows, width = gradient.shape
    slots_dev, size, _ = first_moment.shape
    devices = lax.axis_size("fsdp")
    cols = width // size
    state = jax.ShapeDtypeStruct(first_moment.shape, f32)
    hbm = pl.BlockSpec(memory_space=pltpu.HBM)
    vmem = pl.BlockSpec(memory_space=pltpu.VMEM)
    pieces = pltpu.VMEM((slots_dev, devices, sub_rows, size), f32)
    whole = pltpu.VMEM(first_moment.shape, f32)
    pair = pltpu.VMEM((2, size, size), bf16)
    pairs = pltpu.VMEM((slots_dev, 2, size, size), bf16)
    dma = pltpu.SemaphoreType.DMA
    results = pl.pallas_call(
        kernel,
        out_shape=(pltpu.VMEM((devices * slots_dev, sub_rows, size), f32),) + (whole,) * 4,
        in_specs=[hbm] * 8,
        out_specs=(vmem,) * 5,
        scratch_shapes=[
            pltpu.VMEM((rows_b * cols + 1, sub_rows, size), f32), pieces, pieces, pieces,
            pltpu.VMEM((rows_b, cols), jnp.int32), pltpu.VMEM((8, 128), jnp.int32), pltpu.SMEM((8, 128), jnp.int32),
            whole, whole,
            pairs, pairs, pairs, pairs,
            pair, pair, pair, pair, pltpu.VMEM((size, size), f32),
            pltpu.VMEM((4, 1, 128), f32), pltpu.VMEM((devices, 1, 128), f32),
            pltpu.VMEM((1, 128), f32), pltpu.VMEM((1, 128), f32), pltpu.VMEM((8, size), f32),
            dma((1,)), dma((2,)), dma((6,)), dma((1,)), dma((1,)), dma((2,)), dma((2,)),
            dma((2,)), dma((2,)), dma((2,)), dma((2,)),
        ],
        compiler_params=pltpu.CompilerParams(
            collective_id=0, has_side_effects=True, vmem_limit_bytes=52 * 1024 * 1024
        ),
    )(owner_slot, gradient, first_moment, second_moment, left_basis, right_basis, left_gram, right_gram)
    return pl.pallas_call(
        store,
        out_shape=(jax.ShapeDtypeStruct(gradient.shape, f32), state, state, state, state),
        in_specs=[hbm] + [vmem] * 5,
        out_specs=(hbm,) * 5,
        scratch_shapes=[pltpu.SMEM((rows_b, cols), jnp.int32), dma((1,)), dma((4,)), dma((1,))],
        compiler_params=pltpu.CompilerParams(vmem_limit_bytes=16 * 1024 * 1024),
    )(owner_slot, *results)


def solution(mesh):
    in_specs = (
        P(None, "fsdp", "tp"),
        P("fsdp", None, "tp"),
        P("fsdp", None, "tp"),
        P("fsdp", None, "tp"),
        P("fsdp", None, "tp"),
        P("fsdp", None, "tp"),
        P("fsdp", None, "tp"),
        P(None, "tp"),
    )
    out_specs = (
        P(None, "fsdp", "tp"),
        P("fsdp", None, "tp"),
        P("fsdp", None, "tp"),
        P("fsdp", None, "tp"),
        P("fsdp", None, "tp"),
    )
    return jax.shard_map(local, mesh=mesh, in_specs=in_specs, out_specs=out_specs, check_vma=False)
```
